32 devices in a mesh: seq: 8 (over z, x), mp: 4 (over y, core).
Axes of the slice: x: 2, y: 2, z: 4, core: 2. Of those that a mesh axis runs over, the one named last changes fastest.
Arguments:
- states: bfloat16 [4, 16, 2560], P(None, 'seq', 'mp'), may hold values from -6 to 6
- norm_gain: float32 [2560], replicated, may hold values from 0.5 to 2
- query_gain: float32 [128], replicated, may hold values from 0.7 to 2
- key_gain: float32 [128], replicated, may hold values from 0.7 to 2
- w_query: bfloat16 [2560, 2048], P(None, 'mp'), may hold values from -0.125 to 0.125
- key_matrix: bfloat16 [2560, 512], P(None, 'mp'), may hold values from -0.125 to 0.125
- value_matrix: bfloat16 [2560, 512], P(None, 'mp'), may hold values from -0.125 to 0.125
- w_out: bfloat16 [2048, 2560], P('mp'), may hold values from -0.125 to 0.125
- cached_key_blocks: bfloat16 [128, 256, 512], P('seq', None, 'mp'), may hold values from -216 to 216
- cached_value_blocks: bfloat16 [128, 256, 512], P('seq', None, 'mp'), may hold values from -6 to 6
- req_len: int32 [16], replicated, may hold values from 1 to 2048, as said below
- slot_request: int32 [128], P('seq'), may hold values from 0 to 15, as said below
- slot_block: int32 [128], P('seq'), may hold values from 0 to 7
- slot_empty: int32 [128], P('seq'), may hold values from 0 to 1
Outputs:
- hidden: bfloat16 [4, 16, 2560], P(None, 'seq', 'mp')
- new_keys: bfloat16 [4, 16, 512], P(None, 'seq', 'mp')
- new_values: bfloat16 [4, 16, 512], P(None, 'seq', 'mp')
The draws below stay inside these ranges and needn't reach their ends.
Inputs may be any that keep to these rules, and one draw needn't show every extreme that they name: `req_len`: exactly 12 requests have length 2048; each other request has length at most 511, and one of them exactly that. Slot s holds positions slot_block[s] * 256 onward of request slot_request[s] unless slot_empty[s] = 1. Each block of a request below its length lies in exactly one slot that is not empty. A request of length 2048 has one block on every index of seq; every block of any other request b lies on index b // 2 of seq.
All inputs are finite; a program needn't handle non-finite values.
Results may differ from the reference program's by a relative error of at most 0.0098.
Values may be sent and summed in bfloat16 or wider, within the bound.
A program may use at most 64 MiB of HBM per device.

```python
import math
import jax
import jax.numpy as jnp
from jax import lax

MODEL_WIDTH = 2560
HEAD_SIZE = 128
QUERY_HEADS = 16
KEY_VALUE_HEADS = 4
BLOCK_POSITIONS = 256
STEPS = 4
NLONG = 12
ROWS_DEV = 2
REQUEST_COUNT = 16
SEQUENCE_SLOTS = 16
TOTAL_SLOTS = 128
LONG_LEN = 2048
N_SEQ = 8


def layout(key):
    base_offset = jax.random.fold_in(key, 4242)
    pick_key, length_key, shift_key, order_key = jax.random.split(base_offset, 4)
    request_ids = jnp.arange(REQUEST_COUNT, dtype=jnp.int32)
    long_ids = jax.random.permutation(pick_key, REQUEST_COUNT)[:NLONG].astype(jnp.int32)
    is_long = jnp.any(request_ids[:, None] == long_ids[None, :], axis=1)
    short_len = jax.random.randint(length_key, (REQUEST_COUNT,), 1, 2 * BLOCK_POSITIONS, dtype=jnp.int32)
    first_short = jnp.argmin(jnp.where(is_long, REQUEST_COUNT, request_ids))
    short_len = jnp.where(request_ids == first_short, 2 * BLOCK_POSITIONS - 1, short_len)
    lengths = jnp.where(is_long, LONG_LEN, short_len).astype(jnp.int32)
    devices = jnp.arange(N_SEQ, dtype=jnp.int32)[:, None]
    shifts = jax.random.randint(shift_key, (NLONG,), 0, N_SEQ, dtype=jnp.int32)
    long_request = jnp.broadcast_to(long_ids[None, :], (N_SEQ, NLONG))
    long_block = (devices + shifts[None, :]) % N_SEQ
    long_empty = jnp.zeros((N_SEQ, NLONG), jnp.int32)
    local_slot = jnp.arange(2 * ROWS_DEV, dtype=jnp.int32)[None, :]
    short_request = devices * ROWS_DEV + local_slot // 2
    short_index = jnp.broadcast_to(local_slot % 2, (N_SEQ, 2 * ROWS_DEV))
    owner_len = jnp.take(lengths, short_request)
    owner_long = jnp.take(is_long, short_request)
    short_empty = (owner_long | (short_index == 1) & (owner_len <= BLOCK_POSITIONS)).astype(jnp.int32)
    short_block = jnp.where(short_empty == 1, 0, short_index)
    request_table = jnp.concatenate([long_request, short_request], axis=1)
    block_table = jnp.concatenate([long_block, short_block], axis=1)
    empty_table = jnp.concatenate([long_empty, short_empty], axis=1)

    def shuffle(sub_key):
        return jax.random.permutation(sub_key, SEQUENCE_SLOTS)
    orders = jax.vmap(shuffle)(jax.random.split(order_key, N_SEQ))
    request_flat = jnp.take_along_axis(request_table, orders, axis=1).reshape(-1).astype(jnp.int32)
    block_flat = jnp.take_along_axis(block_table, orders, axis=1).reshape(-1).astype(jnp.int32)
    empty_flat = jnp.take_along_axis(empty_table, orders, axis=1).reshape(-1).astype(jnp.int32)
    return (lengths, request_flat, block_flat, empty_flat)


def draw_req_len(key, part):
    return layout(key)[0]


def draw_slot_request(key, part):
    return layout(key)[1]


def draw_slot_block(key, part):
    return layout(key)[2]


def draw_slot_empty(key, part):
    return layout(key)[3]


def draw_cached_key_blocks(key, part):
    lengths, request_flat, block_flat, empty_flat = layout(key)
    slot_device = jnp.arange(TOTAL_SLOTS, dtype=jnp.int32) // SEQUENCE_SLOTS
    owner_device = request_flat // ROWS_DEV
    slot_long = jnp.take(lengths, request_flat) == LONG_LEN
    across = slot_long & (slot_device == (owner_device + N_SEQ // 2) % N_SEQ) & (empty_flat == 0)
    factor = jnp.where(across, 1.5, 1.0).astype(jnp.float32)[:, None, None]
    base_offset = jax.random.fold_in(key, 31)
    cache_entries = 2.5 * jax.random.truncated_normal(base_offset, -6.0, 6.0, (TOTAL_SLOTS, BLOCK_POSITIONS, KEY_VALUE_HEADS * HEAD_SIZE), jnp.float32)
    cache_entries = cache_entries * factor
    return cache_entries.astype(jnp.bfloat16)


def block_scale(own_key, dims, shards, smallest, top_value):
    loudness = 1.0
    for dim, shards_of in shards:
        draws = jax.random.uniform(jax.random.fold_in(jax.random.fold_in(own_key, 6), dim), (shards_of,), jnp.float32, smallest / len(shards), top_value / len(shards))
        loudness = loudness * jnp.repeat(jnp.exp(draws), dims[dim] // shards_of).reshape((-1,) + (1,) * (len(dims) - 1 - dim))
    return loudness


def noise(stream_key, extent, deviation, bound, cuts=(), held_as=jnp.bfloat16):
    values = deviation * jax.random.normal(stream_key, extent, jnp.float32)
    if cuts:
        values = values * block_scale(stream_key, extent, cuts, -0.22, 0.18)
    return jnp.clip(values, -bound, bound).astype(held_as)


def setup_inputs(seed: int = 0) -> dict:
    seeds = jax.random.split(jax.random.key(seed), 15)
    return {
        "states": noise(seeds[0], (STEPS, REQUEST_COUNT, MODEL_WIDTH), 1.0, 6.0, ((1, 8), (2, 4))),
        "norm_gain": jnp.clip(jnp.exp(jax.random.uniform(seeds[1], (MODEL_WIDTH,), jnp.float32, math.log(0.5), math.log(2.0))), 0.5, 2.0),
        "query_gain": jnp.clip(jnp.exp(jax.random.uniform(seeds[2], (HEAD_SIZE,), jnp.float32, math.log(0.7), math.log(2.0))), 0.7, 2.0),
        "key_gain": jnp.clip(jnp.exp(jax.random.uniform(seeds[3], (HEAD_SIZE,), jnp.float32, math.log(0.7), math.log(2.0))), 0.7, 2.0),
        "w_query": noise(seeds[4], (MODEL_WIDTH, QUERY_HEADS * HEAD_SIZE), MODEL_WIDTH ** -0.5, 0.125, ((1, 4),)),
        "key_matrix": noise(seeds[5], (MODEL_WIDTH, KEY_VALUE_HEADS * HEAD_SIZE), MODEL_WIDTH ** -0.5, 0.125, ((1, 4),)),
        "value_matrix": noise(seeds[6], (MODEL_WIDTH, KEY_VALUE_HEADS * HEAD_SIZE), MODEL_WIDTH ** -0.5, 0.125, ((1, 4),)),
        "w_out": noise(seeds[7], (QUERY_HEADS * HEAD_SIZE, MODEL_WIDTH), (QUERY_HEADS * HEAD_SIZE) ** -0.5, 0.125, ((0, 4),)),
        "cached_key_blocks": draw_cached_key_blocks(jax.random.fold_in(seeds[14], 71), 0),
        "cached_value_blocks": noise(seeds[9], (TOTAL_SLOTS, BLOCK_POSITIONS, KEY_VALUE_HEADS * HEAD_SIZE), 1.0, 6.0, ((0, 8), (2, 4))),
        "req_len": draw_req_len(jax.random.fold_in(seeds[14], 71), 0),
        "slot_request": draw_slot_request(jax.random.fold_in(seeds[14], 71), 0),
        "slot_block": draw_slot_block(jax.random.fold_in(seeds[14], 71), 0),
        "slot_empty": draw_slot_empty(jax.random.fold_in(seeds[14], 71), 0),
    }


ROPE_BASE = 1000000.0
NEGATIVE = -1e+30

def scaled_rms(values, gain):
    return values * lax.rsqrt(lax.optimization_barrier(jnp.mean(values * values, axis=-1, keepdims=True)) + 1e-06) * gain

def rotate(values, positions):
    halfway = values.shape[-1] // 2
    frequency = ROPE_BASE ** (-(jnp.arange(halfway, dtype=jnp.float32) * 2.0) / values.shape[-1])
    angles = positions.astype(jnp.float32)[..., None, None] * frequency
    cosine = jnp.cos(angles)
    sine_part = jnp.sin(angles)
    leading = values[..., :halfway]
    trailing = values[..., halfway:]
    return jnp.concatenate([leading * cosine - trailing * sine_part, trailing * cosine + leading * sine_part], axis=-1)

def project(inputs, positions, norm_gain, query_gain, key_gain, w_query, key_matrix, value_matrix):
    number = inputs.shape[0]
    normed = scaled_rms(inputs.astype(jnp.float32), norm_gain).astype(jnp.bfloat16)
    query_rows = jnp.dot(normed, w_query, preferred_element_type=jnp.float32).reshape(number, -1, HEAD_SIZE)
    keys = jnp.dot(normed, key_matrix, preferred_element_type=jnp.float32).reshape(number, -1, HEAD_SIZE)
    values = jnp.dot(normed, value_matrix, preferred_element_type=jnp.float32).astype(jnp.bfloat16)
    query_rows = rotate(scaled_rms(query_rows, query_gain), positions).reshape(number, -1).astype(jnp.bfloat16)
    keys = rotate(scaled_rms(keys, key_gain), positions).reshape(number, -1).astype(jnp.bfloat16)
    return (query_rows, keys, values)

def reference(states, norm_gain, query_gain, key_gain, w_query, key_matrix, value_matrix, w_out, cached_key_blocks, cached_value_blocks, req_len, slot_request, slot_block, slot_empty):
    head_sharing = QUERY_HEADS // KEY_VALUE_HEADS
    scaling = HEAD_SIZE ** (-0.5)
    offsets = jnp.arange(BLOCK_POSITIONS, dtype=jnp.int32)
    slot_len = jnp.take(req_len, slot_request)
    filled = (slot_empty[:, None] == 0) & (slot_block[:, None] * BLOCK_POSITIONS + offsets[None, :] < slot_len[:, None])
    belongs = (slot_request[None, :] == jnp.arange(REQUEST_COUNT, dtype=jnp.int32)[:, None]) & (slot_empty[None, :] == 0)
    kept_request = jnp.where(slot_empty == 0, slot_request, REQUEST_COUNT).astype(jnp.int32)
    grouped_keys = cached_key_blocks.reshape(N_SEQ, SEQUENCE_SLOTS, BLOCK_POSITIONS, KEY_VALUE_HEADS, HEAD_SIZE)
    grouped_values = cached_value_blocks.reshape(N_SEQ, SEQUENCE_SLOTS, BLOCK_POSITIONS, KEY_VALUE_HEADS, HEAD_SIZE)
    grouped_filled_mask = filled.reshape(N_SEQ, SEQUENCE_SLOTS, BLOCK_POSITIONS)
    grouped_requests = slot_request.reshape(N_SEQ, SEQUENCE_SLOTS)
    current_keys = []
    current_values = []
    results = []
    for sequence_index in range(STEPS):
        positions = req_len + sequence_index
        query_rows, keys, values = project(states[sequence_index], positions, norm_gain, query_gain, key_gain, w_query, key_matrix, value_matrix)
        current_keys.append(keys)
        current_values.append(values)
        query_head_rows = query_rows.reshape(REQUEST_COUNT, KEY_VALUE_HEADS, head_sharing, HEAD_SIZE).astype(jnp.float32)
        earlier_keys = jnp.stack(current_keys).reshape(sequence_index + 1, REQUEST_COUNT, KEY_VALUE_HEADS, HEAD_SIZE).astype(jnp.float32)
        earlier_values = jnp.stack(current_values).reshape(sequence_index + 1, REQUEST_COUNT, KEY_VALUE_HEADS, HEAD_SIZE).astype(jnp.float32)
        fresh_scores = jnp.einsum('bngd,jbnd->bngj', query_head_rows, earlier_keys) * scaling

        def slot_scores(keys_part, filled_part, request_part):
            query_part = jnp.take(query_head_rows, request_part, axis=0)
            raw = jnp.einsum('sngd,sknd->sngk', query_part, keys_part.astype(jnp.float32)) * scaling
            return jnp.where(filled_part[:, None, None, :], raw, NEGATIVE)

        def slot_maximum(operands):
            return lax.optimization_barrier(jnp.max(slot_scores(operands[0], operands[1], operands[2]), axis=-1))
        score_maxima = lax.map(slot_maximum, (grouped_keys, grouped_filled_mask, grouped_requests)).reshape(TOTAL_SLOTS, KEY_VALUE_HEADS, head_sharing)
        cache_top = lax.optimization_barrier(jnp.max(jnp.where(belongs[:, :, None, None], score_maxima[None], NEGATIVE), axis=1))
        overall = jnp.maximum(cache_top, lax.optimization_barrier(jnp.max(fresh_scores, axis=-1)))

        def slot_sums(operands):
            keys_part, values_part, filled_part, request_part = operands
            raw = slot_scores(keys_part, filled_part, request_part)
            reference_top = jnp.take(overall, request_part, axis=0)
            mask_wide = filled_part[:, None, None, :]
            probs = jnp.where(mask_wide, jnp.exp(jnp.where(mask_wide, raw - reference_top[..., None], 0.0)), 0.0)
            rounded = lax.optimization_barrier(probs.astype(jnp.bfloat16)).astype(jnp.float32)
            mixture = jnp.einsum('sngk,sknd->sngd', rounded, values_part.astype(jnp.float32))
            return (lax.optimization_barrier(jnp.sum(probs, axis=-1)), mixture)
        weight_totals, weighted_mixtures = lax.map(slot_sums, (grouped_keys, grouped_values, grouped_filled_mask, grouped_requests))
        weight_totals = weight_totals.reshape(TOTAL_SLOTS, KEY_VALUE_HEADS, head_sharing)
        weighted_mixtures = weighted_mixtures.reshape(TOTAL_SLOTS, KEY_VALUE_HEADS, head_sharing, HEAD_SIZE)
        denominator = jax.ops.segment_sum(weight_totals, kept_request, num_segments=REQUEST_COUNT + 1)[:REQUEST_COUNT]
        mixture = jax.ops.segment_sum(weighted_mixtures, kept_request, num_segments=REQUEST_COUNT + 1)[:REQUEST_COUNT]
        fresh_probs = jnp.exp(fresh_scores - overall[..., None])
        fresh_rounded = lax.optimization_barrier(fresh_probs.astype(jnp.bfloat16)).astype(jnp.float32)
        denominator = denominator + lax.optimization_barrier(jnp.sum(fresh_probs, axis=-1))
        mixture = mixture + jnp.einsum('bngj,jbnd->bngd', fresh_rounded, earlier_values)
        attended = (mixture / denominator[..., None]).astype(jnp.bfloat16).reshape(REQUEST_COUNT, QUERY_HEADS * HEAD_SIZE)
        output = states[sequence_index].astype(jnp.float32) + jnp.dot(attended, w_out, preferred_element_type=jnp.float32)
        results.append(output.astype(jnp.bfloat16))
    return (jnp.stack(results), jnp.stack(current_keys), jnp.stack(current_values))
```

```python
import functools
import math

import jax
import jax.numpy as jnp
from jax import lax
from jax.experimental import pallas as pl
from jax.experimental.pallas import tpu as pltpu
from jax.sharding import PartitionSpec as P

HEAD = 128
EPS = 1e-06
ROPE_BASE = 1000000.0
NEGATIVE = -1e30
F32 = jnp.float32
BF16 = jnp.bfloat16
MESH = pl.DeviceIdType.MESH
UNROLL_UP_TO = 8


def flip(index, k, n):
    total = 0
    bit = 1
    while bit < n:
        a = (index // bit) % 2
        b = (k // bit) % 2
        total = total + (a + b - 2 * a * b) * bit
        bit *= 2
    return total


def loop(low, high, body, carry):
    if high - low < UNROLL_UP_TO:
        for k in range(low, high):
            carry = body(k, carry)
        return carry
    return lax.fori_loop(low, high, body, carry)


def kernel(
    n_seq,
    n_mp,
    states,
    norm_gain,
    query_gain,
    key_gain,
    w_query,
    key_matrix,
    value_matrix,
    w_out,
    cached_keys,
    cached_values,
    req_len,
    slot_request,
    slot_block,
    slot_empty,
    hidden,
    new_keys,
    new_values,
    x_rows,
    x_parts,
    w_all,
    w_out_parts,
    k_all,
    v_all,
    q_rows,
    q_parts,
    o_out,
    o_in,
    st_out,
    st_in,
    att_rows,
    y_out,
    y_in,
    t_rows,
    first_slot,
    first_count,
    second_slot,
    second_count,
    load_sem,
    wo_sem,
    x_send,
    x_recv,
    q_send,
    q_recv,
    o_send,
    o_recv,
    st_send,
    st_recv,
    y_send,
    y_recv,
):
    steps, own, cols = states.shape
    rows = steps * own
    chunks = cols // HEAD
    width = cols * n_mp
    q_width = w_query.shape[1]
    heads = q_width // HEAD
    group = steps * heads
    slots, block_len, _ = cached_keys.shape
    requests = req_len.shape[0]
    scaling = HEAD**-0.5
    my_seq = lax.axis_index("seq")
    my_mp = lax.axis_index("mp")

    barrier = pltpu.get_barrier_semaphore()
    for k in range(1, n_mp):
        pl.semaphore_signal(
            barrier, inc=1, device_id={"mp": flip(my_mp, k, n_mp)}, device_id_type=MESH
        )

    def greet(k, carry):
        pl.semaphore_signal(
            barrier, inc=1, device_id={"seq": flip(my_seq, k, n_seq)}, device_id_type=MESH
        )
        return carry

    loop(1, n_seq, greet, 0)

    loads = [
        pltpu.make_async_copy(w_query, w_all.at[:, 0:q_width], load_sem.at[0]),
        pltpu.make_async_copy(key_matrix, w_all.at[:, q_width : q_width + HEAD], load_sem.at[1]),
        pltpu.make_async_copy(
            value_matrix, w_all.at[:, q_width + HEAD : q_width + 2 * HEAD], load_sem.at[2]
        ),
        pltpu.make_async_copy(cached_keys, k_all, load_sem.at[3]),
        pltpu.make_async_copy(cached_values, v_all, load_sem.at[4]),
    ]
    for k in range(n_mp):
        start = pl.multiple_of(flip(my_mp, k, n_mp) * cols, HEAD)
        loads.append(
            pltpu.make_async_copy(
                w_out.at[:, pl.ds(start, cols)], w_out_parts.at[k], wo_sem.at[k]
            )
        )
    for load in loads:
        load.start()

    for t in range(steps):
        block = states[t].astype(F32)
        for r in range(own):
            x_rows[r * steps + t : r * steps + t + 1, :] = block[r : r + 1, :]
    own_x = x_rows[...]
    pieces = [own_x[:, c * HEAD : (c + 1) * HEAD] for c in range(chunks)]
    padding = x_parts.shape[1] // rows - chunks
    pieces += [jnp.zeros((rows, HEAD), F32)] * padding
    x_parts[my_mp] = jnp.concatenate(pieces, axis=0).astype(BF16)

    pl.semaphore_wait(barrier, n_mp - 1 + n_seq - 1)

    x_copies = []
    for k in range(n_mp - 1, 0, -1):
        x_copies.append(
            pltpu.make_async_remote_copy(
                src_ref=x_parts.at[my_mp],
                dst_ref=x_parts.at[my_mp],
                send_sem=x_send.at[k],
                recv_sem=x_recv.at[k],
                device_id={"mp": flip(my_mp, k, n_mp)},
                device_id_type=MESH,
            )
        )
        x_copies[-1].start()

    owners = []
    for s in range(slots):
        request = slot_request[s]
        used = (slot_empty[s] == 0) & (slot_block[s] * block_len < req_len[request])
        owners.append(jnp.where(used, request, -1))

    def find(b, carry):
        last = jnp.int32(-1)
        earlier = jnp.int32(-1)
        for s in range(slots):
            match = owners[s] == b
            earlier = jnp.where(match, last, earlier)
            last = jnp.where(match, jnp.int32(s), last)
        for found, slot_ref, count_ref in (
            (last, first_slot, first_count),
            (earlier, second_slot, second_count),
        ):
            safe = jnp.maximum(found, 0)
            left = req_len[b] - slot_block[safe] * block_len
            slot_ref[b] = safe
            count_ref[b] = jnp.where(found >= 0, jnp.clip(left, 0, block_len), 0)
        return carry

    lax.fori_loop(0, requests, find, 0)

    row_id = lax.broadcasted_iota(jnp.int32, (rows, HEAD), 0)
    lane_id = lax.broadcasted_iota(jnp.int32, (rows, HEAD), 1)
    position = jnp.zeros((rows, HEAD), jnp.int32)
    for r in range(own):
        length = req_len[my_seq * own + r]
        position = jnp.where(row_id >= r * steps, length + row_id - r * steps, position)
    low_half = lane_id < HEAD // 2
    pair = jnp.where(low_half, lane_id, lane_id - HEAD // 2).astype(F32)
    frequency = jnp.exp(pair * (-2.0 * math.log(ROPE_BASE) / HEAD))
    angle = position.astype(F32) * frequency
    cosine = jnp.cos(angle)
    sine = jnp.sin(angle)
    sine = jnp.where(low_half, -sine, sine)

    def finish_head(values, gain):
        mean = jnp.mean(values * values, axis=-1, keepdims=True)
        values = values * lax.rsqrt(mean + EPS) * gain
        return values * cosine + pltpu.roll(values, HEAD // 2, 1) * sine

    for copy in x_copies:
        copy.wait_recv()
    blocks = []
    square = jnp.zeros((rows, HEAD), F32)
    for m in range(n_mp):
        part = x_parts[m].astype(F32)
        for c in range(chunks):
            piece = part[c * rows : (c + 1) * rows, :]
            blocks.append(piece)
            square = square + piece * piece
    mean = jnp.sum(square, axis=-1, keepdims=True) * (1.0 / width)
    factor = lax.rsqrt(mean + EPS)
    normed = (jnp.concatenate(blocks, axis=1) * factor * norm_gain[...]).astype(BF16)
    for load in loads[:3]:
        load.wait()
    projected = jnp.dot(normed, w_all[...], preferred_element_type=F32)

    for h in range(heads):
        one = finish_head(projected[:, h * HEAD : (h + 1) * HEAD], query_gain[...])
        for r in range(own):
            q_rows[r, h * steps : (h + 1) * steps, :] = one[r * steps : (r + 1) * steps, :]
    for r in range(own):
        q_parts[0, r] = q_rows[r].astype(BF16)

    def query_copy(k):
        return pltpu.make_async_remote_copy(
            src_ref=q_parts.at[0],
            dst_ref=q_parts.at[k],
            send_sem=q_send.at[k],
            recv_sem=q_recv.at[k],
            device_id={"seq": flip(my_seq, k, n_seq)},
            device_id_type=MESH,
        )

    def send_query(i, carry):
        query_copy(n_seq - i).start()
        return carry

    loop(1, n_seq, send_query, 0)

    own_keys = finish_head(projected[:, q_width : q_width + HEAD], key_gain[...])
    own_values = projected[:, q_width + HEAD : q_width + 2 * HEAD]
    for source, target in ((own_keys, new_keys), (own_values, new_values)):
        for r in range(own):
            for t in range(steps):
                t_rows[t * own + r : t * own + r + 1, 0:HEAD] = source[
                    r * steps + t : r * steps + t + 1, :
                ]
        for t in range(steps):
            target[t] = t_rows[t * own : (t + 1) * own, 0:HEAD].astype(BF16)
    own_keys = own_keys.astype(BF16)
    own_values = own_values.astype(BF16)

    for load in loads[3:5]:
        load.wait()

    key_lane = lax.broadcasted_iota(jnp.int32, (group, block_len), 1)
    contract = (((1,), (1,)), ((), ()))

    def masked_scores(query, slot, count):
        scores = lax.dot_general(query, k_all[slot], contract, preferred_element_type=F32)
        return jnp.where(key_lane < count, scores * scaling, NEGATIVE)

    def masked_weights(scores, top, count):
        return jnp.where(key_lane < count, jnp.exp(scores - top), 0.0)

    def row_max(values):
        return jnp.max(values, axis=-1, keepdims=True)

    def row_sum(values):
        return jnp.sum(values, axis=-1, keepdims=True)

    fresh_col = lax.broadcasted_iota(jnp.int32, (group, rows), 1)
    fresh_row = lax.broadcasted_iota(jnp.int32, (group, rows), 0) % steps
    state = []
    for r in range(own):
        b = my_seq * own + r
        query = q_parts[0, r]
        one, one_count = first_slot[b], first_count[b]
        two, two_count = second_slot[b], second_count[b]
        score_one = masked_scores(query, one, one_count)
        score_two = masked_scores(query, two, two_count)
        allowed = (fresh_col >= r * steps) & (fresh_col - r * steps <= fresh_row)
        fresh = lax.dot_general(query, own_keys, contract, preferred_element_type=F32)
        fresh = jnp.where(allowed, fresh * scaling, NEGATIVE)
        top = jnp.maximum(jnp.maximum(row_max(score_one), row_max(score_two)), row_max(fresh))
        weight_one = masked_weights(score_one, top, one_count)
        weight_two = masked_weights(score_two, top, two_count)
        weight_new = jnp.where(allowed, jnp.exp(fresh - top), 0.0)
        total = row_sum(weight_one + weight_two) + row_sum(weight_new)
        mix = (
            jnp.dot(weight_one.astype(BF16), v_all[one], preferred_element_type=F32)
            + jnp.dot(weight_two.astype(BF16), v_all[two], preferred_element_type=F32)
            + jnp.dot(weight_new.astype(BF16), own_values, preferred_element_type=F32)
        )
        state += [top, total, mix]

    stat_lane = lax.broadcasted_iota(jnp.int32, (group, HEAD), 1)
    stat_row = lax.broadcasted_iota(jnp.int32, (group, HEAD), 0)
    at_top = stat_lane == stat_row
    at_total = stat_lane == stat_row + HEAD // 2
    stat_rows = st_out.shape[1]

    def partial_copies(k):
        there = {"seq": flip(my_seq, k, n_seq)}
        return (
            pltpu.make_async_remote_copy(
                src_ref=o_out.at[k],
                dst_ref=o_in.at[k],
                send_sem=o_send.at[k],
                recv_sem=o_recv.at[k],
                device_id=there,
                device_id_type=MESH,
            ),
            pltpu.make_async_remote_copy(
                src_ref=st_out.at[k],
                dst_ref=st_in.at[k],
                send_sem=st_send.at[k],
                recv_sem=st_recv.at[k],
                device_id=there,
                device_id_type=MESH,
            ),
        )

    def serve(k, carry):
        query_copy(k).wait_recv()
        peer = flip(my_seq, k, n_seq)
        lines = []
        for r in range(own):
            b = peer * own + r
            slot, count = first_slot[b], first_count[b]
            scores = masked_scores(q_parts[k, r], slot, count)
            top = row_max(scores)
            weights = masked_weights(scores, top, count)
            total = row_sum(weights)
            mix = jnp.dot(weights.astype(BF16), v_all[slot], preferred_element_type=F32)
            o_out[k, r] = mix.astype(BF16)
            spread = jnp.where(at_top, top, jnp.where(at_total, total, 0.0))
            lines.append(jnp.sum(spread, axis=0, keepdims=True))
        lines.append(jnp.zeros((stat_rows - own, HEAD), F32))
        st_out[k] = jnp.concatenate(lines, axis=0)
        for copy in partial_copies(k):
            copy.start()
        return carry

    loop(1, n_seq, serve, 0)

    def merge(k, carry):
        for copy in partial_copies(k):
            copy.wait_recv()
        carry = list(carry)
        for r in range(own):
            top, total, mix = carry[3 * r : 3 * r + 3]
            line = jnp.broadcast_to(st_in[k, r : r + 1, :], (group, HEAD))
            their_top = row_sum(jnp.where(at_top, line, 0.0))
            their_total = row_sum(jnp.where(at_total, line, 0.0))
            overall = jnp.maximum(top, their_top)
            ours = jnp.exp(top - overall)
            theirs = jnp.exp(their_top - overall)
            carry[3 * r] = overall
            carry[3 * r + 1] = total * ours + their_total * theirs
            carry[3 * r + 2] = mix * ours + o_in[k, r].astype(F32) * theirs
        return tuple(carry)

    state = loop(1, n_seq, merge, tuple(state))

    for r in range(own):
        attended = state[3 * r + 2] / state[3 * r + 1]
        for h in range(heads):
            att_rows[r * steps : (r + 1) * steps, h * HEAD : (h + 1) * HEAD] = attended[
                h * steps : (h + 1) * steps, :
            ]
    attended = att_rows[...].astype(BF16)

    y_copies = []
    for k in range(n_mp - 1, 0, -1):
        loads[5 + k].wait()
        y_out[k] = jnp.dot(attended, w_out_parts[k], preferred_element_type=F32)
        y_copies.append(
            pltpu.make_async_remote_copy(
                src_ref=y_out.at[k],
                dst_ref=y_in.at[k],
                send_sem=y_send.at[k],
                recv_sem=y_recv.at[k],
                device_id={"mp": flip(my_mp, k, n_mp)},
                device_id_type=MESH,
            )
        )
        y_copies[-1].start()
    loads[5].wait()
    summed = jnp.dot(attended, w_out_parts[0], preferred_element_type=F32)
    for copy in y_copies:
        copy.wait_recv()
    for k in range(1, n_mp):
        summed = summed + y_in[k]
    result = x_rows[...] + summed
    for r in range(own):
        for t in range(steps):
            t_rows[t * own + r : t * own + r + 1, :] = result[
                r * steps + t : r * steps + t + 1, :
            ]
    for t in range(steps):
        hidden[t] = t_rows[t * own : (t + 1) * own, :].astype(BF16)

    for copy in x_copies + y_copies:
        copy.wait_send()

    def drain(k, carry):
        query_copy(k).wait_send()
        for copy in partial_copies(k):
            copy.wait_send()
        return carry

    loop(1, n_seq, drain, 0)


def shards(n_seq, n_mp, *args):
    (
        states,
        norm_gain,
        query_gain,
        key_gain,
        w_query,
        key_matrix,
        value_matrix,
        w_out,
        cached_keys,
        cached_values,
        req_len,
        slot_request,
        slot_block,
        slot_empty,
    ) = args
    steps, own, cols = states.shape
    width, q_width = w_query.shape
    heads = q_width // HEAD
    group = steps * heads
    rows = steps * own
    slots, block_len, _ = cached_keys.shape
    requests = req_len.shape[0]
    assert key_matrix.shape[1] == HEAD
    part_rows = -(-(rows * (cols // HEAD)) // 16) * 16
    stat_rows = -(-own // 8) * 8
    vmem = pl.BlockSpec(memory_space=pltpu.VMEM)
    smem = pl.BlockSpec(memory_space=pltpu.SMEM)
    far = pl.BlockSpec(memory_space=pl.ANY)
    dma = pltpu.SemaphoreType.DMA
    return pl.pallas_call(
        functools.partial(kernel, n_seq, n_mp),
        out_shape=(
            jax.ShapeDtypeStruct(states.shape, BF16),
            jax.ShapeDtypeStruct((steps, own, HEAD), BF16),
            jax.ShapeDtypeStruct((steps, own, HEAD), BF16),
        ),
        in_specs=[vmem] * 4 + [far] * 6 + [smem] * 4,
        out_specs=(vmem, vmem, vmem),
        scratch_shapes=[
            pltpu.VMEM((rows, cols), F32),
            pltpu.VMEM((n_mp, part_rows, HEAD), BF16),
            pltpu.VMEM((width, q_width + 2 * HEAD), BF16),
            pltpu.VMEM((n_mp, q_width, cols), BF16),
            pltpu.VMEM((slots, block_len, HEAD), BF16),
            pltpu.VMEM((slots, block_len, HEAD), BF16),
            pltpu.VMEM((own, group, HEAD), F32),
            pltpu.VMEM((n_seq, own, group, HEAD), BF16),
            pltpu.VMEM((n_seq, own, group, HEAD), BF16),
            pltpu.VMEM((n_seq, own, group, HEAD), BF16),
            pltpu.VMEM((n_seq, stat_rows, HEAD), F32),
            pltpu.VMEM((n_seq, stat_rows, HEAD), F32),
            pltpu.VMEM((rows, q_width), F32),
            pltpu.VMEM((n_mp, rows, cols), F32),
            pltpu.VMEM((n_mp, rows, cols), F32),
            pltpu.VMEM((rows, cols), F32),
            pltpu.SMEM((requests,), jnp.int32),
            pltpu.SMEM((requests,), jnp.int32),
            pltpu.SMEM((requests,), jnp.int32),
            pltpu.SMEM((requests,), jnp.int32),
            dma((5,)),
            dma((n_mp,)),
            dma((n_mp,)),
            dma((n_mp,)),
            dma((n_seq,)),
            dma((n_seq,)),
            dma((n_seq,)),
            dma((n_seq,)),
            dma((n_seq,)),
            dma((n_seq,)),
            dma((n_mp,)),
            dma((n_mp,)),
        ],
        compiler_params=pltpu.CompilerParams(
            collective_id=0, has_side_effects=True, vmem_limit_bytes=48 * 1024 * 1024
        ),
    )(
        states,
        norm_gain.reshape(1, -1),
        query_gain.reshape(1, -1),
        key_gain.reshape(1, -1),
        w_query,
        key_matrix,
        value_matrix,
        w_out,
        cached_keys,
        cached_values,
        req_len,
        slot_request,
        slot_block,
        slot_empty,
    )


def solution(mesh):
    placed = (
        P(None, "seq", "mp"),
        P(),
        P(),
        P(),
        P(None, "mp"),
        P(None, "mp"),
        P(None, "mp"),
        P("mp", None),
        P("seq", None, "mp"),
        P("seq", None, "mp"),
        P(),
        P("seq"),
        P("seq"),
        P("seq"),
    )
    return jax.shard_map(
        functools.partial(shards, mesh.shape["seq"], mesh.shape["mp"]),
        mesh=mesh,
        in_specs=placed,
        out_specs=(P(None, "seq", "mp"), P(None, "seq", "mp"), P(None, "seq", "mp")),
        check_vma=False,
    )
```

```python
import functools
import math

import jax
import jax.numpy as jnp
from jax import lax
from jax.experimental import pallas as pl
from jax.experimental.pallas import tpu as pltpu
from jax.sharding import PartitionSpec as P

HEAD = 128
EPS = 1e-06
ROPE_BASE = 1000000.0
NEGATIVE = -1e30
F32 = jnp.float32
BF16 = jnp.bfloat16
MESH = pl.DeviceIdType.MESH
UNROLL_UP_TO = 8


def flip(index, k, n):
    total = 0
    bit = 1
    while bit < n:
        a = (index // bit) % 2
        b = (k // bit) % 2
        total = total + (a + b - 2 * a * b) * bit
        bit *= 2
    return total


def loop(low, high, body, carry):
    if high - low < UNROLL_UP_TO:
        for k in range(low, high):
            carry = body(k, carry)
        return carry
    return lax.fori_loop(low, high, body, carry)


def kernel(
    n_seq,
    n_mp,
    states_far,
    norm_gain_far,
    query_gain_far,
    key_gain_far,
    w_query,
    key_matrix,
    value_matrix,
    w_out,
    cached_keys,
    cached_values,
    req_len_far,
    slot_request_far,
    slot_block_far,
    slot_empty_far,
    hidden,
    new_keys,
    new_values,
    states,
    norm_gain,
    query_gain,
    key_gain,
    req_len,
    slot_request,
    slot_block,
    slot_empty,
    x_rows,
    x_parts,
    w_all,
    w_out_parts,
    k_all,
    v_all,
    q_rows,
    q_parts,
    o_out,
    o_in,
    st_out,
    st_in,
    att_rows,
    y_out,
    y_in,
    t_rows,
    first_slot,
    first_count,
    second_slot,
    second_count,
    small_sem,
    load_sem,
    wo_sem,
    x_send,
    x_recv,
    q_send,
    q_recv,
    o_send,
    o_recv,
    st_send,
    st_recv,
    y_send,
    y_recv,
):
    steps, own, cols = states.shape
    rows = steps * own
    chunks = cols // HEAD
    width = cols * n_mp
    q_width = w_query.shape[1]
    heads = q_width // HEAD
    group = steps * heads
    slots, block_len, _ = cached_keys.shape
    requests = req_len.shape[0]
    scaling = HEAD**-0.5
    my_seq = lax.axis_index("seq")
    my_mp = lax.axis_index("mp")

    smalls = [
        pltpu.make_async_copy(source, target, small_sem.at[i])
        for i, (source, target) in enumerate(
            (
                (states_far, states),
                (req_len_far, req_len),
                (slot_request_far, slot_request),
                (slot_block_far, slot_block),
                (slot_empty_far, slot_empty),
                (norm_gain_far, norm_gain),
                (query_gain_far, query_gain),
                (key_gain_far, key_gain),
            )
        )
    ]
    for small in smalls:
        small.start()

    barrier = pltpu.get_barrier_semaphore()
    for k in range(1, n_mp):
        pl.semaphore_signal(
            barrier, inc=1, device_id={"mp": flip(my_mp, k, n_mp)}, device_id_type=MESH
        )

    def greet(k, carry):
        pl.semaphore_signal(
            barrier, inc=1, device_id={"seq": flip(my_seq, k, n_seq)}, device_id_type=MESH
        )
        return carry

    loop(1, n_seq, greet, 0)

    loads = [
        pltpu.make_async_copy(w_query, w_all.at[:, 0:q_width], load_sem.at[0]),
        pltpu.make_async_copy(key_matrix, w_all.at[:, q_width : q_width + HEAD], load_sem.at[1]),
        pltpu.make_async_copy(
            value_matrix, w_all.at[:, q_width + HEAD : q_width + 2 * HEAD], load_sem.at[2]
        ),
        pltpu.make_async_copy(cached_keys, k_all, load_sem.at[3]),
        pltpu.make_async_copy(cached_values, v_all, load_sem.at[4]),
    ]
    for k in range(n_mp):
        start = pl.multiple_of(flip(my_mp, k, n_mp) * cols, HEAD)
        loads.append(
            pltpu.make_async_copy(
                w_out.at[:, pl.ds(start, cols)], w_out_parts.at[k], wo_sem.at[k]
            )
        )
    for load in loads:
        load.start()

    smalls[0].wait()
    for t in range(steps):
        block = states[t].astype(F32)
        for r in range(own):
            x_rows[r * steps + t : r * steps + t + 1, :] = block[r : r + 1, :]
    own_x = x_rows[...]
    pieces = [own_x[:, c * HEAD : (c + 1) * HEAD] for c in range(chunks)]
    padding = x_parts.shape[1] // rows - chunks
    pieces += [jnp.zeros((rows, HEAD), F32)] * padding
    x_parts[my_mp] = jnp.concatenate(pieces, axis=0).astype(BF16)

    pl.semaphore_wait(barrier, n_mp - 1 + n_seq - 1)

    x_copies = []
    for k in range(n_mp - 1, 0, -1):
        x_copies.append(
            pltpu.make_async_remote_copy(
                src_ref=x_parts.at[my_mp],
                dst_ref=x_parts.at[my_mp],
                send_sem=x_send.at[k],
                recv_sem=x_recv.at[k],
                device_id={"mp": flip(my_mp, k, n_mp)},
                device_id_type=MESH,
            )
        )
        x_copies[-1].start()

    for small in smalls[1:]:
        small.wait()

    owners = []
    for s in range(slots):
        request = slot_request[s]
        used = (slot_empty[s] == 0) & (slot_block[s] * block_len < req_len[request])
        owners.append(jnp.where(used, request, -1))

    def find(b, carry):
        last = jnp.int32(-1)
        earlier = jnp.int32(-1)
        for s in range(slots):
            match = owners[s] == b
            earlier = jnp.where(match, last, earlier)
            last = jnp.where(match, jnp.int32(s), last)
        for found, slot_ref, count_ref in (
            (last, first_slot, first_count),
            (earlier, second_slot, second_count),
        ):
            safe = jnp.maximum(found, 0)
            left = req_len[b] - slot_block[safe] * block_len
            slot_ref[b] = safe
            count_ref[b] = jnp.where(found >= 0, jnp.clip(left, 0, block_len), 0)
        return carry

    lax.fori_loop(0, requests, find, 0)

    row_id = lax.broadcasted_iota(jnp.int32, (rows, HEAD), 0)
    lane_id = lax.broadcasted_iota(jnp.int32, (rows, HEAD), 1)
    position = jnp.zeros((rows, HEAD), jnp.int32)
    for r in range(own):
        length = req_len[my_seq * own + r]
        position = jnp.where(row_id >= r * steps, length + row_id - r * steps, position)
    low_half = lane_id < HEAD // 2
    pair = jnp.where(low_half, lane_id, lane_id - HEAD // 2).astype(F32)
    frequency = jnp.exp(pair * (-2.0 * math.log(ROPE_BASE) / HEAD))
    angle = position.astype(F32) * frequency
    cosine = jnp.cos(angle)
    sine = jnp.sin(angle)
    sine = jnp.where(low_half, -sine, sine)

    def finish_head(values, gain):
        mean = jnp.mean(values * values, axis=-1, keepdims=True)
        values = values * lax.rsqrt(mean + EPS) * gain
        return values * cosine + pltpu.roll(values, HEAD // 2, 1) * sine

    for copy in x_copies:
        copy.wait_recv()
    blocks = []
    square = jnp.zeros((rows, HEAD), F32)
    for m in range(n_mp):
        part = x_parts[m].astype(F32)
        for c in range(chunks):
            piece = part[c * rows : (c + 1) * rows, :]
            blocks.append(piece)
            square = square + piece * piece
    mean = jnp.sum(square, axis=-1, keepdims=True) * (1.0 / width)
    factor = lax.rsqrt(mean + EPS)
    gains = norm_gain[...]
    normed = jnp.concatenate(
        [piece * factor * gains[i : i + 1, :] for i, piece in enumerate(blocks)], axis=1
    ).astype(BF16)
    for load in loads[:3]:
        load.wait()
    projected = jnp.dot(normed, w_all[...], preferred_element_type=F32)

    for h in range(heads):
        one = finish_head(projected[:, h * HEAD : (h + 1) * HEAD], query_gain[...])
        for r in range(own):
            q_rows[r, h * steps : (h + 1) * steps, :] = one[r * steps : (r + 1) * steps, :]
    for r in range(own):
        q_parts[0, r] = q_rows[r].astype(BF16)

    def query_copy(k):
        return pltpu.make_async_remote_copy(
            src_ref=q_parts.at[0],
            dst_ref=q_parts.at[k],
            send_sem=q_send.at[k],
            recv_sem=q_recv.at[k],
            device_id={"seq": flip(my_seq, k, n_seq)},
            device_id_type=MESH,
        )

    def send_query(i, carry):
        query_copy(n_seq - i).start()
        return carry

    loop(1, n_seq, send_query, 0)

    own_keys = finish_head(projected[:, q_width : q_width + HEAD], key_gain[...])
    own_values = projected[:, q_width + HEAD : q_width + 2 * HEAD]
    for source, target in ((own_keys, new_keys), (own_values, new_values)):
        for r in range(own):
            for t in range(steps):
                t_rows[t * own + r : t * own + r + 1, 0:HEAD] = source[
                    r * steps + t : r * steps + t + 1, :
                ]
        for t in range(steps):
            target[t] = t_rows[t * own : (t + 1) * own, 0:HEAD].astype(BF16)
    own_keys = own_keys.astype(BF16)
    own_values = own_values.astype(BF16)

    for load in loads[3:5]:
        load.wait()

    key_lane = lax.broadcasted_iota(jnp.int32, (group, block_len), 1)
    contract = (((1,), (1,)), ((), ()))

    def masked_scores(query, slot, count):
        scores = lax.dot_general(query, k_all[slot], contract, preferred_element_type=F32)
        return jnp.where(key_lane < count, scores * scaling, NEGATIVE)

    def masked_weights(scores, top, count):
        return jnp.where(key_lane < count, jnp.exp(scores - top), 0.0)

    def row_max(values):
        return jnp.max(values, axis=-1, keepdims=True)

    def row_sum(values):
        return jnp.sum(values, axis=-1, keepdims=True)

    fresh_col = lax.broadcasted_iota(jnp.int32, (group, rows), 1)
    fresh_row = lax.broadcasted_iota(jnp.int32, (group, rows), 0) % steps
    state = []
    for r in range(own):
        b = my_seq * own + r
        query = q_parts[0, r]
        one, one_count = first_slot[b], first_count[b]
        two, two_count = second_slot[b], second_count[b]
        score_one = masked_scores(query, one, one_count)
        score_two = masked_scores(query, two, two_count)
        allowed = (fresh_col >= r * steps) & (fresh_col - r * steps <= fresh_row)
        fresh = lax.dot_general(query, own_keys, contract, preferred_element_type=F32)
        fresh = jnp.where(allowed, fresh * scaling, NEGATIVE)
        top = jnp.maximum(jnp.maximum(row_max(score_one), row_max(score_two)), row_max(fresh))
        weight_one = masked_weights(score_one, top, one_count)
        weight_two = masked_weights(score_two, top, two_count)
        weight_new = jnp.where(allowed, jnp.exp(fresh - top), 0.0)
        total = row_sum(weight_one + weight_two) + row_sum(weight_new)
        mix = (
            jnp.dot(weight_one.astype(BF16), v_all[one], preferred_element_type=F32)
            + jnp.dot(weight_two.astype(BF16), v_all[two], preferred_element_type=F32)
            + jnp.dot(weight_new.astype(BF16), own_values, preferred_element_type=F32)
        )
        state += [top, total, mix]

    stat_lane = lax.broadcasted_iota(jnp.int32, (group, HEAD), 1)
    stat_row = lax.broadcasted_iota(jnp.int32, (group, HEAD), 0)
    at_top = stat_lane == stat_row
    at_total = stat_lane == stat_row + HEAD // 2
    stat_rows = st_out.shape[1]

    def partial_copies(k):
        there = {"seq": flip(my_seq, k, n_seq)}
        return (
            pltpu.make_async_remote_copy(
                src_ref=o_out.at[k],
                dst_ref=o_in.at[k],
                send_sem=o_send.at[k],
                recv_sem=o_recv.at[k],
                device_id=there,
                device_id_type=MESH,
            ),
            pltpu.make_async_remote_copy(
                src_ref=st_out.at[k],
                dst_ref=st_in.at[k],
                send_sem=st_send.at[k],
                recv_sem=st_recv.at[k],
                device_id=there,
                device_id_type=MESH,
            ),
        )

    def serve(ks):
        jobs = []
        for k in ks:
            query_copy(k).wait_recv()
        for k in ks:
            peer = flip(my_seq, k, n_seq)
            for r in range(own):
                b = peer * own + r
                jobs.append((k, r, first_slot[b], first_count[b]))
        scores = [masked_scores(q_parts[k, r], slot, count) for k, r, slot, count in jobs]
        tops = [row_max(score) for score in scores]
        weights = [
            masked_weights(score, top, job[3]) for score, top, job in zip(scores, tops, jobs)
        ]
        totals = [row_sum(weight) for weight in weights]
        lines = []
        for (k, r, slot, _), weight, top, total in zip(jobs, weights, tops, totals):
            mix = jnp.dot(weight.astype(BF16), v_all[slot], preferred_element_type=F32)
            o_out[k, r] = mix.astype(BF16)
            spread = jnp.where(at_top, top, jnp.where(at_total, total, 0.0))
            lines.append(jnp.sum(spread, axis=0, keepdims=True))
        blank = jnp.zeros((stat_rows - own, HEAD), F32)
        for i, k in enumerate(ks):
            st_out[k] = jnp.concatenate(lines[i * own : (i + 1) * own] + [blank], axis=0)
        for k in ks:
            for copy in partial_copies(k):
                copy.start()

    def merge(ks, carry):
        for k in ks:
            for copy in partial_copies(k):
                copy.wait_recv()
        carry = list(carry)
        for r in range(own):
            tops, totals, mixes = ([item] for item in carry[3 * r : 3 * r + 3])
            for k in ks:
                line = jnp.broadcast_to(st_in[k, r : r + 1, :], (group, HEAD))
                tops.append(row_sum(jnp.where(at_top, line, 0.0)))
                totals.append(row_sum(jnp.where(at_total, line, 0.0)))
                mixes.append(o_in[k, r].astype(F32))
            overall = functools.reduce(jnp.maximum, tops)
            factors = [jnp.exp(top - overall) for top in tops]
            carry[3 * r] = overall
            carry[3 * r + 1] = sum(total * f for total, f in zip(totals, factors))
            carry[3 * r + 2] = sum(mix * f for mix, f in zip(mixes, factors))
        return tuple(carry)

    state = tuple(state)
    if n_seq <= UNROLL_UP_TO:
        groups = [range(1, n_seq // 2), range(n_seq // 2, n_seq)]
        for ks in groups:
            serve(ks)
        for ks in groups:
            state = merge(ks, state)
    else:

        def serve_one(k, carry):
            serve([k])
            return carry

        lax.fori_loop(1, n_seq, serve_one, 0)
        state = lax.fori_loop(1, n_seq, lambda k, carry: merge([k], carry), state)

    for r in range(own):
        attended = state[3 * r + 2] / state[3 * r + 1]
        for h in range(heads):
            att_rows[r * steps : (r + 1) * steps, h * HEAD : (h + 1) * HEAD] = attended[
                h * steps : (h + 1) * steps, :
            ]
    attended = att_rows[...].astype(BF16)

    y_copies = []
    for k in range(n_mp - 1, 0, -1):
        loads[5 + k].wait()
        y_out[k] = jnp.dot(attended, w_out_parts[k], preferred_element_type=F32)
        y_copies.append(
            pltpu.make_async_remote_copy(
                src_ref=y_out.at[k],
                dst_ref=y_in.at[k],
                send_sem=y_send.at[k],
                recv_sem=y_recv.at[k],
                device_id={"mp": flip(my_mp, k, n_mp)},
                device_id_type=MESH,
            )
        )
        y_copies[-1].start()
    loads[5].wait()
    summed = jnp.dot(attended, w_out_parts[0], preferred_element_type=F32)
    for copy in y_copies:
        copy.wait_recv()
    for k in range(1, n_mp):
        summed = summed + y_in[k]
    result = x_rows[...] + summed
    for r in range(own):
        for t in range(steps):
            t_rows[t * own + r : t * own + r + 1, :] = result[
                r * steps + t : r * steps + t + 1, :
            ]
    for t in range(steps):
        hidden[t] = t_rows[t * own : (t + 1) * own, :].astype(BF16)

    for copy in x_copies + y_copies:
        copy.wait_send()

    def drain(k, carry):
        query_copy(k).wait_send()
        for copy in partial_copies(k):
            copy.wait_send()
        return carry

    loop(1, n_seq, drain, 0)


def shards(n_seq, n_mp, *args):
    (
        states,
        norm_gain,
        query_gain,
        key_gain,
        w_query,
        key_matrix,
        value_matrix,
        w_out,
        cached_keys,
        cached_values,
        req_len,
        slot_request,
        slot_block,
        slot_empty,
    ) = args
    steps, own, cols = states.shape
    width, q_width = w_query.shape
    heads = q_width // HEAD
    group = steps * heads
    rows = steps * own
    slots, block_len, _ = cached_keys.shape
    requests = req_len.shape[0]
    assert key_matrix.shape[1] == HEAD
    part_rows = -(-(rows * (cols // HEAD)) // 16) * 16
    stat_rows = -(-own // 8) * 8
    vmem = pl.BlockSpec(memory_space=pltpu.VMEM)
    far = pl.BlockSpec(memory_space=pltpu.HBM)
    dma = pltpu.SemaphoreType.DMA
    return pl.pallas_call(
        functools.partial(kernel, n_seq, n_mp),
        out_shape=(
            jax.ShapeDtypeStruct(states.shape, BF16),
            jax.ShapeDtypeStruct((steps, own, HEAD), BF16),
            jax.ShapeDtypeStruct((steps, own, HEAD), BF16),
        ),
        in_specs=[far] * 14,
        out_specs=(vmem, vmem, vmem),
        scratch_shapes=[
            pltpu.VMEM(states.shape, BF16),
            pltpu.VMEM((width // HEAD, HEAD), F32),
            pltpu.VMEM((1, HEAD), F32),
            pltpu.VMEM((1, HEAD), F32),
            pltpu.SMEM((requests,), jnp.int32),
            pltpu.SMEM((slots,), jnp.int32),
            pltpu.SMEM((slots,), jnp.int32),
            pltpu.SMEM((slots,), jnp.int32),
            pltpu.VMEM((rows, cols), F32),
            pltpu.VMEM((n_mp, part_rows, HEAD), BF16),
            pltpu.VMEM((width, q_width + 2 * HEAD), BF16),
            pltpu.VMEM((n_mp, q_width, cols), BF16),
            pltpu.VMEM((slots, block_len, HEAD), BF16),
            pltpu.VMEM((slots, block_len, HEAD), BF16),
            pltpu.VMEM((own, group, HEAD), F32),
            pltpu.VMEM((n_seq, own, group, HEAD), BF16),
            pltpu.VMEM((n_seq, own, group, HEAD), BF16),
            pltpu.VMEM((n_seq, own, group, HEAD), BF16),
            pltpu.VMEM((n_seq, stat_rows, HEAD), F32),
            pltpu.VMEM((n_seq, stat_rows, HEAD), F32),
            pltpu.VMEM((rows, q_width), F32),
            pltpu.VMEM((n_mp, rows, cols), F32),
            pltpu.VMEM((n_mp, rows, cols), F32),
            pltpu.VMEM((rows, cols), F32),
            pltpu.SMEM((requests,), jnp.int32),
            pltpu.SMEM((requests,), jnp.int32),
            pltpu.SMEM((requests,), jnp.int32),
            pltpu.SMEM((requests,), jnp.int32),
            dma((8,)),
            dma((5,)),
            dma((n_mp,)),
            dma((n_mp,)),
            dma((n_mp,)),
            dma((n_seq,)),
            dma((n_seq,)),
            dma((n_seq,)),
            dma((n_seq,)),
            dma((n_seq,)),
            dma((n_seq,)),
            dma((n_mp,)),
            dma((n_mp,)),
        ],
        compiler_params=pltpu.CompilerParams(
            collective_id=0, has_side_effects=True, vmem_limit_bytes=63 * 1024 * 1024
        ),
    )(
        states,
        norm_gain.reshape(-1, HEAD),
        query_gain.reshape(1, -1),
        key_gain.reshape(1, -1),
        w_query,
        key_matrix,
        value_matrix,
        w_out,
        cached_keys,
        cached_values,
        req_len,
        slot_request,
        slot_block,
        slot_empty,
    )


def solution(mesh):
    placed = (
        P(None, "seq", "mp"),
        P(),
        P(),
        P(),
        P(None, "mp"),
        P(None, "mp"),
        P(None, "mp"),
        P("mp", None),
        P("seq", None, "mp"),
        P("seq", None, "mp"),
        P(),
        P("seq"),
        P("seq"),
        P("seq"),
    )
    return jax.shard_map(
        functools.partial(shards, mesh.shape["seq"], mesh.shape["mp"]),
        mesh=mesh,
        in_specs=placed,
        out_specs=(P(None, "seq", "mp"), P(None, "seq", "mp"), P(None, "seq", "mp")),
        check_vma=False,
    )
```

```python
import functools
import math

import jax
import jax.numpy as jnp
from jax import lax
from jax.experimental import pallas as pl
from jax.experimental.pallas import tpu as pltpu
from jax.sharding import PartitionSpec as P

HEAD = 128
EPS = 1e-06
ROPE_BASE = 1000000.0
NEGATIVE = -1e30
F32 = jnp.float32
BF16 = jnp.bfloat16
MESH = pl.DeviceIdType.MESH
UNROLL_UP_TO = 8


def flip(index, k, n):
    total = 0
    bit = 1
    while bit < n:
        a = (index // bit) % 2
        b = (k // bit) % 2
        total = total + (a + b - 2 * a * b) * bit
        bit *= 2
    return total


def loop(low, high, body, carry):
    if high - low < UNROLL_UP_TO:
        for k in range(low, high):
            carry = body(k, carry)
        return carry
    return lax.fori_loop(low, high, body, carry)


def kernel(
    n_seq,
    n_mp,
    states_far,
    norm_gain_far,
    query_gain_far,
    key_gain_far,
    w_query,
    key_matrix,
    value_matrix,
    w_out,
    cached_keys,
    cached_values,
    req_len_far,
    slot_request_far,
    slot_block_far,
    slot_empty_far,
    hidden,
    new_keys,
    new_values,
    states,
    norm_gain,
    query_gain,
    key_gain,
    req_len,
    slot_request,
    slot_block,
    slot_empty,
    x_rows,
    x_parts,
    w_all,
    w_out_parts,
    k_all,
    v_all,
    q_rows,
    q_parts,
    o_out,
    o_in,
    st_out,
    st_in,
    att_rows,
    y_out,
    y_in,
    t_rows,
    first_slot,
    first_count,
    second_slot,
    second_count,
    small_sem,
    load_sem,
    wo_sem,
    x_send,
    x_recv,
    q_send,
    q_recv,
    o_send,
    o_recv,
    st_send,
    st_recv,
    y_send,
    y_recv,
):
    steps, own, cols = states.shape
    rows = steps * own
    chunks = cols // HEAD
    width = cols * n_mp
    q_width = w_query.shape[1]
    heads = q_width // HEAD
    group = steps * heads
    slots, block_len, _ = cached_keys.shape
    requests = req_len.shape[0]
    scaling = HEAD**-0.5
    my_seq = lax.axis_index("seq")
    my_mp = lax.axis_index("mp")

    smalls = [
        pltpu.make_async_copy(source, target, small_sem.at[i])
        for i, (source, target) in enumerate(
            (
                (states_far, states),
                (req_len_far, req_len),
                (slot_request_far, slot_request),
                (slot_block_far, slot_block),
                (slot_empty_far, slot_empty),
                (norm_gain_far, norm_gain),
                (query_gain_far, query_gain),
                (key_gain_far, key_gain),
            )
        )
    ]
    for small in smalls:
        small.start()

    barrier = pltpu.get_barrier_semaphore()
    for k in range(1, n_mp):
        pl.semaphore_signal(
            barrier, inc=1, device_id={"mp": flip(my_mp, k, n_mp)}, device_id_type=MESH
        )

    def greet(k, carry):
        pl.semaphore_signal(
            barrier, inc=1, device_id={"seq": flip(my_seq, k, n_seq)}, device_id_type=MESH
        )
        return carry

    loop(1, n_seq, greet, 0)

    loads = [
        pltpu.make_async_copy(w_query, w_all.at[:, 0:q_width], load_sem.at[0]),
        pltpu.make_async_copy(key_matrix, w_all.at[:, q_width : q_width + HEAD], load_sem.at[1]),
        pltpu.make_async_copy(
            value_matrix, w_all.at[:, q_width + HEAD : q_width + 2 * HEAD], load_sem.at[2]
        ),
        pltpu.make_async_copy(cached_keys, k_all, load_sem.at[3]),
        pltpu.make_async_copy(cached_values, v_all, load_sem.at[4]),
    ]
    for k in range(n_mp):
        start = pl.multiple_of(flip(my_mp, k, n_mp) * cols, HEAD)
        loads.append(
            pltpu.make_async_copy(
                w_out.at[:, pl.ds(start, cols)], w_out_parts.at[k], wo_sem.at[k]
            )
        )
    for load in loads[:3]:
        load.start()

    smalls[0].wait()
    for t in range(steps):
        block = states[t].astype(F32)
        for r in range(own):
            x_rows[r * steps + t : r * steps + t + 1, :] = block[r : r + 1, :]
    own_x = x_rows[...]
    padding = x_parts.shape[1] // rows - chunks

    def fold(wide):
        pieces = [wide[:, c * HEAD : (c + 1) * HEAD] for c in range(chunks)]
        pieces += [jnp.zeros((rows, HEAD), F32)] * padding
        return jnp.concatenate(pieces, axis=0).astype(BF16)

    x_parts[my_mp] = fold(own_x)

    pl.semaphore_wait(barrier, n_mp - 1 + n_seq - 1)

    x_copies = []
    for k in range(n_mp - 1, 0, -1):
        x_copies.append(
            pltpu.make_async_remote_copy(
                src_ref=x_parts.at[my_mp],
                dst_ref=x_parts.at[my_mp],
                send_sem=x_send.at[k],
                recv_sem=x_recv.at[k],
                device_id={"mp": flip(my_mp, k, n_mp)},
                device_id_type=MESH,
            )
        )
        x_copies[-1].start()
    for load in loads[3:]:
        load.start()

    for small in smalls[1:]:
        small.wait()

    owners = []
    for s in range(slots):
        request = slot_request[s]
        used = (slot_empty[s] == 0) & (slot_block[s] * block_len < req_len[request])
        owners.append(jnp.where(used, request, -1))

    def find(b, carry):
        last = jnp.int32(-1)
        earlier = jnp.int32(-1)
        for s in range(slots):
            match = owners[s] == b
            earlier = jnp.where(match, last, earlier)
            last = jnp.where(match, jnp.int32(s), last)
        for found, slot_ref, count_ref in (
            (last, first_slot, first_count),
            (earlier, second_slot, second_count),
        ):
            safe = jnp.maximum(found, 0)
            left = req_len[b] - slot_block[safe] * block_len
            slot_ref[b] = safe
            count_ref[b] = jnp.where(found >= 0, jnp.clip(left, 0, block_len), 0)
        return carry

    lax.fori_loop(0, requests, find, 0)

    row_id = lax.broadcasted_iota(jnp.int32, (rows, HEAD), 0)
    lane_id = lax.broadcasted_iota(jnp.int32, (rows, HEAD), 1)
    position = jnp.zeros((rows, HEAD), jnp.int32)
    for r in range(own):
        length = req_len[my_seq * own + r]
        position = jnp.where(row_id >= r * steps, length + row_id - r * steps, position)
    low_half = lane_id < HEAD // 2
    pair = jnp.where(low_half, lane_id, lane_id - HEAD // 2).astype(F32)
    frequency = jnp.exp(pair * (-2.0 * math.log(ROPE_BASE) / HEAD))
    angle = position.astype(F32) * frequency
    cosine = jnp.cos(angle)
    sine = jnp.sin(angle)
    sine = jnp.where(low_half, -sine, sine)

    def finish_head(values, gain):
        mean = jnp.mean(values * values, axis=-1, keepdims=True)
        values = values * lax.rsqrt(mean + EPS) * gain
        return values * cosine + pltpu.roll(values, HEAD // 2, 1) * sine

    for copy in x_copies:
        copy.wait_recv()
    blocks = []
    square = jnp.zeros((rows, HEAD), F32)
    for m in range(n_mp):
        part = x_parts[m].astype(F32)
        for c in range(chunks):
            piece = part[c * rows : (c + 1) * rows, :]
            blocks.append(piece)
            square = square + piece * piece
    mean = jnp.sum(square, axis=-1, keepdims=True) * (1.0 / width)
    factor = lax.rsqrt(mean + EPS)
    gains = norm_gain[...]
    normed = jnp.concatenate(
        [piece * factor * gains[i : i + 1, :] for i, piece in enumerate(blocks)], axis=1
    ).astype(BF16)
    for load in loads[:3]:
        load.wait()
    projected = jnp.dot(normed, w_all[...], preferred_element_type=F32)

    for h in range(heads):
        one = finish_head(projected[:, h * HEAD : (h + 1) * HEAD], query_gain[...])
        for r in range(own):
            q_rows[r, h * steps : (h + 1) * steps, :] = one[r * steps : (r + 1) * steps, :]
    for r in range(own):
        q_parts[0, r] = q_rows[r].astype(BF16)

    def query_copy(k):
        return pltpu.make_async_remote_copy(
            src_ref=q_parts.at[0],
            dst_ref=q_parts.at[k],
            send_sem=q_send.at[k],
            recv_sem=q_recv.at[k],
            device_id={"seq": flip(my_seq, k, n_seq)},
            device_id_type=MESH,
        )

    def send_query(i, carry):
        query_copy(n_seq - i).start()
        return carry

    loop(1, n_seq, send_query, 0)

    own_keys = finish_head(projected[:, q_width : q_width + HEAD], key_gain[...])
    own_values = projected[:, q_width + HEAD : q_width + 2 * HEAD]
    for source, target in ((own_keys, new_keys), (own_values, new_values)):
        for r in range(own):
            for t in range(steps):
                t_rows[t * own + r : t * own + r + 1, 0:HEAD] = source[
                    r * steps + t : r * steps + t + 1, :
                ]
        for t in range(steps):
            target[t] = t_rows[t * own : (t + 1) * own, 0:HEAD].astype(BF16)
    own_keys = own_keys.astype(BF16)
    own_values = own_values.astype(BF16)

    for load in loads[3:5]:
        load.wait()

    key_lane = lax.broadcasted_iota(jnp.int32, (group, block_len), 1)
    contract = (((1,), (1,)), ((), ()))

    def masked_scores(query, slot, count):
        scores = lax.dot_general(query, k_all[slot], contract, preferred_element_type=F32)
        return jnp.where(key_lane < count, scores * scaling, NEGATIVE)

    def masked_weights(scores, top, count):
        return jnp.where(key_lane < count, jnp.exp(scores - top), 0.0)

    def row_max(values):
        return jnp.max(values, axis=-1, keepdims=True)

    def row_sum(values):
        return jnp.sum(values, axis=-1, keepdims=True)

    fresh_col = lax.broadcasted_iota(jnp.int32, (group, rows), 1)
    fresh_row = lax.broadcasted_iota(jnp.int32, (group, rows), 0) % steps
    state = []
    for r in range(own):
        b = my_seq * own + r
        query = q_parts[0, r]
        one, one_count = first_slot[b], first_count[b]
        two, two_count = second_slot[b], second_count[b]
        score_one = masked_scores(query, one, one_count)
        score_two = masked_scores(query, two, two_count)
        allowed = (fresh_col >= r * steps) & (fresh_col - r * steps <= fresh_row)
        fresh = lax.dot_general(query, own_keys, contract, preferred_element_type=F32)
        fresh = jnp.where(allowed, fresh * scaling, NEGATIVE)
        top = jnp.maximum(jnp.maximum(row_max(score_one), row_max(score_two)), row_max(fresh))
        weight_one = masked_weights(score_one, top, one_count)
        weight_two = masked_weights(score_two, top, two_count)
        weight_new = jnp.where(allowed, jnp.exp(fresh - top), 0.0)
        total = row_sum(weight_one + weight_two) + row_sum(weight_new)
        mix = (
            jnp.dot(weight_one.astype(BF16), v_all[one], preferred_element_type=F32)
            + jnp.dot(weight_two.astype(BF16), v_all[two], preferred_element_type=F32)
            + jnp.dot(weight_new.astype(BF16), own_values, preferred_element_type=F32)
        )
        state += [top, total, mix]

    stat_lane = lax.broadcasted_iota(jnp.int32, (group, HEAD), 1)
    stat_row = lax.broadcasted_iota(jnp.int32, (group, HEAD), 0)
    at_top = stat_lane == stat_row
    at_total = stat_lane == stat_row + HEAD // 2

    def partial_copies(k):
        there = {"seq": flip(my_seq, k, n_seq)}
        return (
            pltpu.make_async_remote_copy(
                src_ref=o_out.at[k],
                dst_ref=o_in.at[k],
                send_sem=o_send.at[k],
                recv_sem=o_recv.at[k],
                device_id=there,
                device_id_type=MESH,
            ),
            pltpu.make_async_remote_copy(
                src_ref=st_out.at[k],
                dst_ref=st_in.at[k],
                send_sem=st_send.at[k],
                recv_sem=st_recv.at[k],
                device_id=there,
                device_id_type=MESH,
            ),
        )

    def serve(ks):
        jobs = []
        for k in ks:
            query_copy(k).wait_recv()
        for k in ks:
            peer = flip(my_seq, k, n_seq)
            for r in range(own):
                b = peer * own + r
                jobs.append((k, r, first_slot[b], first_count[b]))
        scores = [masked_scores(q_parts[k, r], slot, count) for k, r, slot, count in jobs]
        tops = [row_max(score) for score in scores]
        weights = [
            masked_weights(score, top, job[3]) for score, top, job in zip(scores, tops, jobs)
        ]
        totals = [row_sum(weight) for weight in weights]
        lines = []
        for (k, r, slot, _), weight, top, total in zip(jobs, weights, tops, totals):
            mix = jnp.dot(weight.astype(BF16), v_all[slot], preferred_element_type=F32)
            o_out[k, r] = mix.astype(BF16)
            spread = jnp.where(at_top, top, jnp.where(at_total, total, 0.0))
            lines.append(jnp.sum(spread, axis=0, keepdims=True))
        for line, (k, r, _, _) in zip(lines, jobs):
            st_out[k, r : r + 1, :] = line
        for k in ks:
            for copy in partial_copies(k):
                copy.start()

    def merge(ks, carry):
        for k in ks:
            for copy in partial_copies(k):
                copy.wait_recv()
        carry = list(carry)
        for r in range(own):
            tops, totals, mixes = ([item] for item in carry[3 * r : 3 * r + 3])
            for k in ks:
                line = jnp.broadcast_to(st_in[k, r : r + 1, :], (group, HEAD))
                tops.append(row_sum(jnp.where(at_top, line, 0.0)))
                totals.append(row_sum(jnp.where(at_total, line, 0.0)))
                mixes.append(o_in[k, r].astype(F32))
            overall = functools.reduce(jnp.maximum, tops)
            factors = [jnp.exp(top - overall) for top in tops]
            carry[3 * r] = overall
            carry[3 * r + 1] = sum(total * f for total, f in zip(totals, factors))
            carry[3 * r + 2] = sum(mix * f for mix, f in zip(mixes, factors))
        return tuple(carry)

    state = tuple(state)
    if n_seq <= UNROLL_UP_TO:
        groups = [range(1, n_seq // 2), range(n_seq // 2, n_seq)]
        for ks in groups:
            serve(ks)
        for ks in groups:
            state = merge(ks, state)
    else:

        def serve_one(k, carry):
            serve([k])
            return carry

        lax.fori_loop(1, n_seq, serve_one, 0)
        state = lax.fori_loop(1, n_seq, lambda k, carry: merge([k], carry), state)

    for r in range(own):
        attended = state[3 * r + 2] / state[3 * r + 1]
        for h in range(heads):
            att_rows[r * steps : (r + 1) * steps, h * HEAD : (h + 1) * HEAD] = attended[
                h * steps : (h + 1) * steps, :
            ]
    attended = att_rows[...].astype(BF16)

    y_copies = []
    for k in range(n_mp - 1, 0, -1):
        loads[5 + k].wait()
        y_out[k] = fold(jnp.dot(attended, w_out_parts[k], preferred_element_type=F32))
        y_copies.append(
            pltpu.make_async_remote_copy(
                src_ref=y_out.at[k],
                dst_ref=y_in.at[k],
                send_sem=y_send.at[k],
                recv_sem=y_recv.at[k],
                device_id={"mp": flip(my_mp, k, n_mp)},
                device_id_type=MESH,
            )
        )
        y_copies[-1].start()
    loads[5].wait()
    summed = jnp.dot(attended, w_out_parts[0], preferred_element_type=F32)
    summed = x_rows[...] + summed

    for copy in x_copies:
        copy.wait_send()

    def drain(k, carry):
        query_copy(k).wait_send()
        for copy in partial_copies(k):
            copy.wait_send()
        return carry

    loop(1, n_seq, drain, 0)

    for copy in y_copies:
        copy.wait_recv()
    for k in range(1, n_mp):
        folded = y_in[k].astype(F32)
        summed = summed + jnp.concatenate(
            [folded[c * rows : (c + 1) * rows, :] for c in range(chunks)], axis=1
        )
    for r in range(own):
        for t in range(steps):
            t_rows[t * own + r : t * own + r + 1, :] = summed[
                r * steps + t : r * steps + t + 1, :
            ]
    for t in range(steps):
        hidden[t] = t_rows[t * own : (t + 1) * own, :].astype(BF16)
    for copy in y_copies:
        copy.wait_send()


def write_out(*refs):
    count = len(refs) // 2
    sem = refs[-1]
    copies = [
        pltpu.make_async_copy(refs[i], refs[count + i], sem.at[i]) for i in range(count)
    ]
    for copy in copies:
        copy.start()
    for copy in copies:
        copy.wait()


def shards(n_seq, n_mp, *args):
    (
        states,
        norm_gain,
        query_gain,
        key_gain,
        w_query,
        key_matrix,
        value_matrix,
        w_out,
        cached_keys,
        cached_values,
        req_len,
        slot_request,
        slot_block,
        slot_empty,
    ) = args
    steps, own, cols = states.shape
    width, q_width = w_query.shape
    heads = q_width // HEAD
    group = steps * heads
    rows = steps * own
    slots, block_len, _ = cached_keys.shape
    requests = req_len.shape[0]
    assert key_matrix.shape[1] == HEAD
    part_rows = -(-(rows * (cols // HEAD)) // 16) * 16
    vmem = pl.BlockSpec(memory_space=pltpu.VMEM)
    far = pl.BlockSpec(memory_space=pltpu.HBM)
    dma = pltpu.SemaphoreType.DMA
    results = pl.pallas_call(
        functools.partial(kernel, n_seq, n_mp),
        out_shape=(
            pltpu.VMEM(states.shape, BF16),
            pltpu.VMEM((steps, own, HEAD), BF16),
            pltpu.VMEM((steps, own, HEAD), BF16),
        ),
        in_specs=[far] * 14,
        out_specs=(vmem, vmem, vmem),
        scratch_shapes=[
            pltpu.VMEM(states.shape, BF16),
            pltpu.VMEM((width // HEAD, HEAD), F32),
            pltpu.VMEM((1, HEAD), F32),
            pltpu.VMEM((1, HEAD), F32),
            pltpu.SMEM((requests,), jnp.int32),
            pltpu.SMEM((slots,), jnp.int32),
            pltpu.SMEM((slots,), jnp.int32),
            pltpu.SMEM((slots,), jnp.int32),
            pltpu.VMEM((rows, cols), F32),
            pltpu.VMEM((n_mp, part_rows, HEAD), BF16),
            pltpu.VMEM((width, q_width + 2 * HEAD), BF16),
            pltpu.VMEM((n_mp, q_width, cols), BF16),
            pltpu.VMEM((slots, block_len, HEAD), BF16),
            pltpu.VMEM((slots, block_len, HEAD), BF16),
            pltpu.VMEM((own, group, HEAD), F32),
            pltpu.VMEM((n_seq, own, group, HEAD), BF16),
            pltpu.VMEM((n_seq, own, group, HEAD), BF16),
            pltpu.VMEM((n_seq, own, group, HEAD), BF16),
            pltpu.VMEM((n_seq, own, HEAD), F32),
            pltpu.VMEM((n_seq, own, HEAD), F32),
            pltpu.VMEM((rows, q_width), F32),
            pltpu.VMEM((n_mp, part_rows, HEAD), BF16),
            pltpu.VMEM((n_mp, part_rows, HEAD), BF16),
            pltpu.VMEM((rows, cols), F32),
            pltpu.SMEM((requests,), jnp.int32),
            pltpu.SMEM((requests,), jnp.int32),
            pltpu.SMEM((requests,), jnp.int32),
            pltpu.SMEM((requests,), jnp.int32),
            dma((8,)),
            dma((5,)),
            dma((n_mp,)),
            dma((n_mp,)),
            dma((n_mp,)),
            dma((n_seq,)),
            dma((n_seq,)),
            dma((n_seq,)),
            dma((n_seq,)),
            dma((n_seq,)),
            dma((n_seq,)),
            dma((n_mp,)),
            dma((n_mp,)),
        ],
        compiler_params=pltpu.CompilerParams(
            collective_id=0, has_side_effects=True, vmem_limit_bytes=63 * 1024 * 1024
        ),
    )(
        states,
        norm_gain.reshape(-1, HEAD),
        query_gain.reshape(1, -1),
        key_gain.reshape(1, -1),
        w_query,
        key_matrix,
        value_matrix,
        w_out,
        cached_keys,
        cached_values,
        req_len,
        slot_request,
        slot_block,
        slot_empty,
    )
    return pl.pallas_call(
        write_out,
        out_shape=tuple(jax.ShapeDtypeStruct(x.shape, x.dtype) for x in results),
        in_specs=[vmem] * 3,
        out_specs=(far,) * 3,
        scratch_shapes=[dma((3,))],
    )(*results)


def solution(mesh):
    placed = (
        P(None, "seq", "mp"),
        P(),
        P(),
        P(),
        P(None, "mp"),
        P(None, "mp"),
        P(None, "mp"),
        P("mp", None),
        P("seq", None, "mp"),
        P("seq", None, "mp"),
        P(),
        P("seq"),
        P("seq"),
        P("seq"),
    )
    return jax.shard_map(
        functools.partial(shards, mesh.shape["seq"], mesh.shape["mp"]),
        mesh=mesh,
        in_specs=placed,
        out_specs=(P(None, "seq", "mp"), P(None, "seq", "mp"), P(None, "seq", "mp")),
        check_vma=False,
    )
```

```python
import functools
import math

import jax
import jax.numpy as jnp
from jax import lax
from jax.experimental import pallas as pl
from jax.experimental.pallas import tpu as pltpu
from jax.sharding import PartitionSpec as P

HEAD = 128
EPS = 1e-06
ROPE_BASE = 1000000.0
NEGATIVE = -1e30
F32 = jnp.float32
BF16 = jnp.bfloat16
MESH = pl.DeviceIdType.MESH
UNROLL_UP_TO = 8


def flip(index, k, n):
    total = 0
    bit = 1
    while bit < n:
        a = (index // bit) % 2
        b = (k // bit) % 2
        total = total + (a + b - 2 * a * b) * bit
        bit *= 2
    return total


def loop(low, high, body, carry):
    if high - low < UNROLL_UP_TO:
        for k in range(low, high):
            carry = body(k, carry)
        return carry
    return lax.fori_loop(low, high, body, carry)


def kernel(
    n_seq,
    n_mp,
    states_far,
    norm_gain_far,
    query_gain_far,
    key_gain_far,
    w_query,
    key_matrix,
    value_matrix,
    w_out,
    cached_keys,
    cached_values,
    req_len_far,
    slot_request_far,
    slot_block_far,
    slot_empty_far,
    hidden,
    new_keys,
    new_values,
    x_raw,
    norm_gain,
    query_gain,
    key_gain,
    req_len,
    slot_request,
    slot_block,
    slot_empty,
    x_rows,
    w_all,
    w_out_parts,
    k_all,
    v_all,
    q_rows,
    q_parts,
    o_out,
    o_in,
    st_out,
    st_in,
    att_rows,
    y_out,
    y_in,
    t_rows,
    first_slot,
    first_count,
    second_slot,
    second_count,
    small_sem,
    load_sem,
    wo_sem,
    x_send,
    x_recv,
    q_send,
    q_recv,
    o_send,
    o_recv,
    st_send,
    st_recv,
    y_send,
    y_recv,
):
    steps, own, cols = states_far.shape
    rows = steps * own
    chunks = cols // HEAD
    width = cols * n_mp
    q_width = w_query.shape[1]
    heads = q_width // HEAD
    group = steps * heads
    slots, block_len, _ = cached_keys.shape
    requests = req_len.shape[0]
    scaling = HEAD**-0.5
    my_seq = lax.axis_index("seq")
    my_mp = lax.axis_index("mp")

    smalls = [
        pltpu.make_async_copy(source, target, small_sem.at[i])
        for i, (source, target) in enumerate(
            (
                (states_far, x_raw.at[lax.axis_index("mp")]),
                (req_len_far, req_len),
                (slot_request_far, slot_request),
                (slot_block_far, slot_block),
                (slot_empty_far, slot_empty),
                (norm_gain_far, norm_gain),
                (query_gain_far, query_gain),
                (key_gain_far, key_gain),
            )
        )
    ]
    for small in smalls:
        small.start()

    barrier = pltpu.get_barrier_semaphore()
    for k in range(1, n_mp):
        pl.semaphore_signal(
            barrier, inc=1, device_id={"mp": flip(my_mp, k, n_mp)}, device_id_type=MESH
        )

    def greet(k, carry):
        pl.semaphore_signal(
            barrier, inc=1, device_id={"seq": flip(my_seq, k, n_seq)}, device_id_type=MESH
        )
        return carry

    loop(1, n_seq, greet, 0)

    loads = [
        pltpu.make_async_copy(w_query, w_all.at[:, 0:q_width], load_sem.at[0]),
        pltpu.make_async_copy(key_matrix, w_all.at[:, q_width : q_width + HEAD], load_sem.at[1]),
        pltpu.make_async_copy(
            value_matrix, w_all.at[:, q_width + HEAD : q_width + 2 * HEAD], load_sem.at[2]
        ),
        pltpu.make_async_copy(cached_keys, k_all, load_sem.at[3]),
        pltpu.make_async_copy(cached_values, v_all, load_sem.at[4]),
    ]
    for k in range(n_mp):
        start = pl.multiple_of(flip(my_mp, k, n_mp) * cols, HEAD)
        loads.append(
            pltpu.make_async_copy(
                w_out.at[:, pl.ds(start, cols)], w_out_parts.at[k], wo_sem.at[k]
            )
        )
    for load in loads[:3]:
        load.start()

    padding = y_out.shape[1] // rows - chunks

    def fold(wide):
        pieces = [wide[:, c * HEAD : (c + 1) * HEAD] for c in range(chunks)]
        pieces += [jnp.zeros((rows, HEAD), F32)] * padding
        return jnp.concatenate(pieces, axis=0).astype(BF16)

    pl.semaphore_wait(barrier, n_mp - 1 + n_seq - 1)

    x_copies = []
    for k in range(n_mp - 1, 0, -1):
        x_copies.append(
            pltpu.make_async_remote_copy(
                src_ref=states_far,
                dst_ref=x_raw.at[my_mp],
                send_sem=x_send.at[k],
                recv_sem=x_recv.at[k],
                device_id={"mp": flip(my_mp, k, n_mp)},
                device_id_type=MESH,
            )
        )
        x_copies[-1].start()
    for load in loads[3:]:
        load.start()

    for small in smalls:
        small.wait()

    owners = []
    for s in range(slots):
        request = slot_request[s]
        used = (slot_empty[s] == 0) & (slot_block[s] * block_len < req_len[request])
        owners.append(jnp.where(used, request, -1))

    def find(b, carry):
        last = jnp.int32(-1)
        earlier = jnp.int32(-1)
        for s in range(slots):
            match = owners[s] == b
            earlier = jnp.where(match, last, earlier)
            last = jnp.where(match, jnp.int32(s), last)
        for found, slot_ref, count_ref in (
            (last, first_slot, first_count),
            (earlier, second_slot, second_count),
        ):
            safe = jnp.maximum(found, 0)
            left = req_len[b] - slot_block[safe] * block_len
            slot_ref[b] = safe
            count_ref[b] = jnp.where(found >= 0, jnp.clip(left, 0, block_len), 0)
        return carry

    lax.fori_loop(0, requests, find, 0)

    row_id = lax.broadcasted_iota(jnp.int32, (rows, HEAD), 0)
    lane_id = lax.broadcasted_iota(jnp.int32, (rows, HEAD), 1)
    position = jnp.zeros((rows, HEAD), jnp.int32)
    for r in range(own):
        length = req_len[my_seq * own + r]
        position = jnp.where(row_id >= r * steps, length + row_id - r * steps, position)
    low_half = lane_id < HEAD // 2
    pair = jnp.where(low_half, lane_id, lane_id - HEAD // 2).astype(F32)
    frequency = jnp.exp(pair * (-2.0 * math.log(ROPE_BASE) / HEAD))
    angle = position.astype(F32) * frequency
    cosine = jnp.cos(angle)
    sine = jnp.sin(angle)
    sine = jnp.where(low_half, -sine, sine)

    def finish_head(values, gain):
        mean = jnp.mean(values * values, axis=-1, keepdims=True)
        values = values * lax.rsqrt(mean + EPS) * gain
        return values * cosine + pltpu.roll(values, HEAD // 2, 1) * sine

    for copy in x_copies:
        copy.wait_recv()
    for m in range(n_mp):
        for t in range(steps):
            block = x_raw[m, t].astype(F32)
            for r in range(own):
                x_rows[r * steps + t : r * steps + t + 1, m * cols : (m + 1) * cols] = block[
                    r : r + 1, :
                ]
    blocks = [x_rows[:, c * HEAD : (c + 1) * HEAD] for c in range(n_mp * chunks)]
    square = sum(piece * piece for piece in blocks)
    mean = jnp.sum(square, axis=-1, keepdims=True) * (1.0 / width)
    factor = lax.rsqrt(mean + EPS)
    gains = norm_gain[...]
    normed = jnp.concatenate(
        [piece * factor * gains[i : i + 1, :] for i, piece in enumerate(blocks)], axis=1
    ).astype(BF16)
    for load in loads[:3]:
        load.wait()
    projected = jnp.dot(normed, w_all[...], preferred_element_type=F32)

    for h in range(heads):
        one = finish_head(projected[:, h * HEAD : (h + 1) * HEAD], query_gain[...])
        for r in range(own):
            q_rows[r, h * steps : (h + 1) * steps, :] = one[r * steps : (r + 1) * steps, :]
    for r in range(own):
        q_parts[0, r] = q_rows[r].astype(BF16)

    def query_copy(k):
        return pltpu.make_async_remote_copy(
            src_ref=q_parts.at[0],
            dst_ref=q_parts.at[k],
            send_sem=q_send.at[k],
            recv_sem=q_recv.at[k],
            device_id={"seq": flip(my_seq, k, n_seq)},
            device_id_type=MESH,
        )

    def send_query(i, carry):
        query_copy(n_seq - i).start()
        return carry

    loop(1, n_seq, send_query, 0)

    own_keys = finish_head(projected[:, q_width : q_width + HEAD], key_gain[...])
    own_values = projected[:, q_width + HEAD : q_width + 2 * HEAD]
    for source, target in ((own_keys, new_keys), (own_values, new_values)):
        for r in range(own):
            for t in range(steps):
                t_rows[t * own + r : t * own + r + 1, 0:HEAD] = source[
                    r * steps + t : r * steps + t + 1, :
                ]
        for t in range(steps):
            target[t] = t_rows[t * own : (t + 1) * own, 0:HEAD].astype(BF16)
    own_keys = own_keys.astype(BF16)
    own_values = own_values.astype(BF16)

    for load in loads[3:5]:
        load.wait()

    key_lane = lax.broadcasted_iota(jnp.int32, (group, block_len), 1)
    contract = (((1,), (1,)), ((), ()))

    def masked_scores(query, slot, count):
        scores = lax.dot_general(query, k_all[slot], contract, preferred_element_type=F32)
        return jnp.where(key_lane < count, scores * scaling, NEGATIVE)

    def masked_weights(scores, top, count):
        return jnp.where(key_lane < count, jnp.exp(scores - top), 0.0)

    def row_max(values):
        return jnp.max(values, axis=-1, keepdims=True)

    def row_sum(values):
        return jnp.sum(values, axis=-1, keepdims=True)

    fresh_col = lax.broadcasted_iota(jnp.int32, (group, rows), 1)
    fresh_row = lax.broadcasted_iota(jnp.int32, (group, rows), 0) % steps
    state = []
    for r in range(own):
        b = my_seq * own + r
        query = q_parts[0, r]
        one, one_count = first_slot[b], first_count[b]
        two, two_count = second_slot[b], second_count[b]
        score_one = masked_scores(query, one, one_count)
        score_two = masked_scores(query, two, two_count)
        allowed = (fresh_col >= r * steps) & (fresh_col - r * steps <= fresh_row)
        fresh = lax.dot_general(query, own_keys, contract, preferred_element_type=F32)
        fresh = jnp.where(allowed, fresh * scaling, NEGATIVE)
        top = jnp.maximum(jnp.maximum(row_max(score_one), row_max(score_two)), row_max(fresh))
        weight_one = masked_weights(score_one, top, one_count)
        weight_two = masked_weights(score_two, top, two_count)
        weight_new = jnp.where(allowed, jnp.exp(fresh - top), 0.0)
        total = row_sum(weight_one + weight_two) + row_sum(weight_new)
        mix = (
            jnp.dot(weight_one.astype(BF16), v_all[one], preferred_element_type=F32)
            + jnp.dot(weight_two.astype(BF16), v_all[two], preferred_element_type=F32)
            + jnp.dot(weight_new.astype(BF16), own_values, preferred_element_type=F32)
        )
        state += [top, total, mix]

    stat_lane = lax.broadcasted_iota(jnp.int32, (group, HEAD), 1)
    stat_row = lax.broadcasted_iota(jnp.int32, (group, HEAD), 0)
    at_top = stat_lane == stat_row
    at_total = stat_lane == stat_row + HEAD // 2

    def partial_copies(k):
        there = {"seq": flip(my_seq, k, n_seq)}
        return (
            pltpu.make_async_remote_copy(
                src_ref=o_out.at[k],
                dst_ref=o_in.at[k],
                send_sem=o_send.at[k],
                recv_sem=o_recv.at[k],
                device_id=there,
                device_id_type=MESH,
            ),
            pltpu.make_async_remote_copy(
                src_ref=st_out.at[k],
                dst_ref=st_in.at[k],
                send_sem=st_send.at[k],
                recv_sem=st_recv.at[k],
                device_id=there,
                device_id_type=MESH,
            ),
        )

    def serve(ks):
        jobs = []
        for k in ks:
            query_copy(k).wait_recv()
        for k in ks:
            peer = flip(my_seq, k, n_seq)
            for r in range(own):
                b = peer * own + r
                jobs.append((k, r, first_slot[b], first_count[b]))
        scores = [masked_scores(q_parts[k, r], slot, count) for k, r, slot, count in jobs]
        tops = [row_max(score) for score in scores]
        weights = [
            masked_weights(score, top, job[3]) for score, top, job in zip(scores, tops, jobs)
        ]
        totals = [row_sum(weight) for weight in weights]
        lines = []
        for (k, r, slot, _), weight, top, total in zip(jobs, weights, tops, totals):
            mix = jnp.dot(weight.astype(BF16), v_all[slot], preferred_element_type=F32)
            o_out[k, r] = mix.astype(BF16)
            spread = jnp.where(at_top, top, jnp.where(at_total, total, 0.0))
            lines.append(jnp.sum(spread, axis=0, keepdims=True))
        for line, (k, r, _, _) in zip(lines, jobs):
            st_out[k, r : r + 1, :] = line
        for k in ks:
            for copy in partial_copies(k):
                copy.start()

    def merge(ks, carry):
        for k in ks:
            for copy in partial_copies(k):
                copy.wait_recv()
        carry = list(carry)
        for r in range(own):
            tops, totals, mixes = ([item] for item in carry[3 * r : 3 * r + 3])
            for k in ks:
                line = jnp.broadcast_to(st_in[k, r : r + 1, :], (group, HEAD))
                tops.append(row_sum(jnp.where(at_top, line, 0.0)))
                totals.append(row_sum(jnp.where(at_total, line, 0.0)))
                mixes.append(o_in[k, r].astype(F32))
            overall = functools.reduce(jnp.maximum, tops)
            factors = [jnp.exp(top - overall) for top in tops]
            carry[3 * r] = overall
            carry[3 * r + 1] = sum(total * f for total, f in zip(totals, factors))
            carry[3 * r + 2] = sum(mix * f for mix, f in zip(mixes, factors))
        return tuple(carry)

    state = tuple(state)
    if n_seq <= UNROLL_UP_TO:
        groups = [range(1, n_seq // 2), range(n_seq // 2, n_seq)]
        for ks in groups:
            serve(ks)
        for ks in groups:
            state = merge(ks, state)
    else:

        def serve_one(k, carry):
            serve([k])
            return carry

        lax.fori_loop(1, n_seq, serve_one, 0)
        state = lax.fori_loop(1, n_seq, lambda k, carry: merge([k], carry), state)

    for r in range(own):
        attended = state[3 * r + 2] / state[3 * r + 1]
        for h in range(heads):
            att_rows[r * steps : (r + 1) * steps, h * HEAD : (h + 1) * HEAD] = attended[
                h * steps : (h + 1) * steps, :
            ]
    attended = att_rows[...].astype(BF16)

    y_copies = []
    for k in range(n_mp - 1, 0, -1):
        loads[5 + k].wait()
        y_out[k] = fold(jnp.dot(attended, w_out_parts[k], preferred_element_type=F32))
        y_copies.append(
            pltpu.make_async_remote_copy(
                src_ref=y_out.at[k],
                dst_ref=y_in.at[k],
                send_sem=y_send.at[k],
                recv_sem=y_recv.at[k],
                device_id={"mp": flip(my_mp, k, n_mp)},
                device_id_type=MESH,
            )
        )
        y_copies[-1].start()
    loads[5].wait()
    summed = jnp.dot(attended, w_out_parts[0], preferred_element_type=F32)
    own_start = pl.multiple_of(my_mp * cols, HEAD)
    summed = x_rows[:, pl.ds(own_start, cols)] + summed

    for copy in x_copies:
        copy.wait_send()

    def drain(k, carry):
        query_copy(k).wait_send()
        for copy in partial_copies(k):
            copy.wait_send()
        return carry

    loop(1, n_seq, drain, 0)

    for copy in y_copies:
        copy.wait_recv()
    for k in range(1, n_mp):
        folded = y_in[k].astype(F32)
        summed = summed + jnp.concatenate(
            [folded[c * rows : (c + 1) * rows, :] for c in range(chunks)], axis=1
        )
    for r in range(own):
        for t in range(steps):
            t_rows[t * own + r : t * own + r + 1, :] = summed[
                r * steps + t : r * steps + t + 1, :
            ]
    for t in range(steps):
        hidden[t] = t_rows[t * own : (t + 1) * own, :].astype(BF16)
    for copy in y_copies:
        copy.wait_send()


def write_out(*refs):
    count = len(refs) // 2
    sem = refs[-1]
    copies = [
        pltpu.make_async_copy(refs[i], refs[count + i], sem.at[i]) for i in range(count)
    ]
    for copy in copies:
        copy.start()
    for copy in copies:
        copy.wait()


def shards(n_seq, n_mp, *args):
    (
        states,
        norm_gain,
        query_gain,
        key_gain,
        w_query,
        key_matrix,
        value_matrix,
        w_out,
        cached_keys,
        cached_values,
        req_len,
        slot_request,
        slot_block,
        slot_empty,
    ) = args
    steps, own, cols = states.shape
    width, q_width = w_query.shape
    heads = q_width // HEAD
    group = steps * heads
    rows = steps * own
    slots, block_len, _ = cached_keys.shape
    requests = req_len.shape[0]
    assert key_matrix.shape[1] == HEAD
    part_rows = -(-(rows * (cols // HEAD)) // 16) * 16
    vmem = pl.BlockSpec(memory_space=pltpu.VMEM)
    far = pl.BlockSpec(memory_space=pltpu.HBM)
    dma = pltpu.SemaphoreType.DMA
    results = pl.pallas_call(
        functools.partial(kernel, n_seq, n_mp),
        out_shape=(
            pltpu.VMEM(states.shape, BF16),
            pltpu.VMEM((steps, own, HEAD), BF16),
            pltpu.VMEM((steps, own, HEAD), BF16),
        ),
        in_specs=[far] * 14,
        out_specs=(vmem, vmem, vmem),
        scratch_shapes=[
            pltpu.VMEM((n_mp,) + states.shape, BF16),
            pltpu.VMEM((width // HEAD, HEAD), F32),
            pltpu.VMEM((1, HEAD), F32),
            pltpu.VMEM((1, HEAD), F32),
            pltpu.SMEM((requests,), jnp.int32),
            pltpu.SMEM((slots,), jnp.int32),
            pltpu.SMEM((slots,), jnp.int32),
            pltpu.SMEM((slots,), jnp.int32),
            pltpu.VMEM((rows, width), F32),
            pltpu.VMEM((width, q_width + 2 * HEAD), BF16),
            pltpu.VMEM((n_mp, q_width, cols), BF16),
            pltpu.VMEM((slots, block_len, HEAD), BF16),
            pltpu.VMEM((slots, block_len, HEAD), BF16),
            pltpu.VMEM((own, group, HEAD), F32),
            pltpu.VMEM((n_seq, own, group, HEAD), BF16),
            pltpu.VMEM((n_seq, own, group, HEAD), BF16),
            pltpu.VMEM((n_seq, own, group, HEAD), BF16),
            pltpu.VMEM((n_seq, own, HEAD), F32),
            pltpu.VMEM((n_seq, own, HEAD), F32),
            pltpu.VMEM((rows, q_width), F32),
            pltpu.VMEM((n_mp, part_rows, HEAD), BF16),
            pltpu.VMEM((n_mp, part_rows, HEAD), BF16),
            pltpu.VMEM((rows, cols), F32),
            pltpu.SMEM((requests,), jnp.int32),
            pltpu.SMEM((requests,), jnp.int32),
            pltpu.SMEM((requests,), jnp.int32),
            pltpu.SMEM((requests,), jnp.int32),
            dma((8,)),
            dma((5,)),
            dma((n_mp,)),
            dma((n_mp,)),
            dma((n_mp,)),
            dma((n_seq,)),
            dma((n_seq,)),
            dma((n_seq,)),
            dma((n_seq,)),
            dma((n_seq,)),
            dma((n_seq,)),
            dma((n_mp,)),
            dma((n_mp,)),
        ],
        compiler_params=pltpu.CompilerParams(
            collective_id=0, has_side_effects=True, vmem_limit_bytes=63 * 1024 * 1024
        ),
    )(
        states,
        norm_gain.reshape(-1, HEAD),
        query_gain.reshape(1, -1),
        key_gain.reshape(1, -1),
        w_query,
        key_matrix,
        value_matrix,
        w_out,
        cached_keys,
        cached_values,
        req_len,
        slot_request,
        slot_block,
        slot_empty,
    )
    return pl.pallas_call(
        write_out,
        out_shape=tuple(jax.ShapeDtypeStruct(x.shape, x.dtype) for x in results),
        in_specs=[vmem] * 3,
        out_specs=(far,) * 3,
        scratch_shapes=[dma((3,))],
        compiler_params=pltpu.CompilerParams(vmem_limit_bytes=1024 * 1024),
    )(*results)


def solution(mesh):
    placed = (
        P(None, "seq", "mp"),
        P(),
        P(),
        P(),
        P(None, "mp"),
        P(None, "mp"),
        P(None, "mp"),
        P("mp", None),
        P("seq", None, "mp"),
        P("seq", None, "mp"),
        P(),
        P("seq"),
        P("seq"),
        P("seq"),
    )
    return jax.shard_map(
        functools.partial(shards, mesh.shape["seq"], mesh.shape["mp"]),
        mesh=mesh,
        in_specs=placed,
        out_specs=(P(None, "seq", "mp"), P(None, "seq", "mp"), P(None, "seq", "mp")),
        check_vma=False,
    )
```

```python
import functools
import math

import jax
import jax.numpy as jnp
from jax import lax
from jax.experimental import pallas as pl
from jax.experimental.pallas import tpu as pltpu
from jax.sharding import PartitionSpec as P

HEAD = 128
EPS = 1e-06
ROPE_BASE = 1000000.0
NEGATIVE = -1e30
F32 = jnp.float32
BF16 = jnp.bfloat16
MESH = pl.DeviceIdType.MESH
UNROLL_UP_TO = 8


def flip(index, k, n):
    total = 0
    bit = 1
    while bit < n:
        a = (index // bit) % 2
        b = (k // bit) % 2
        total = total + (a + b - 2 * a * b) * bit
        bit *= 2
    return total


def loop(low, high, body, carry):
    if high - low < UNROLL_UP_TO:
        for k in range(low, high):
            carry = body(k, carry)
        return carry
    return lax.fori_loop(low, high, body, carry)


def kernel(
    n_seq,
    n_mp,
    states_far,
    norm_gain_far,
    query_gain_far,
    key_gain_far,
    w_query,
    key_matrix,
    value_matrix,
    w_out,
    cached_keys,
    cached_values,
    req_len_far,
    slot_request_far,
    slot_block_far,
    slot_empty_far,
    hidden,
    new_keys,
    new_values,
    x_raw,
    norm_gain,
    query_gain,
    key_gain,
    req_len,
    slot_request,
    slot_block,
    slot_empty,
    x_rows,
    w_all,
    w_out_parts,
    k_all,
    v_all,
    q_rows,
    q_parts,
    o_out,
    o_in,
    st_out,
    st_in,
    att_rows,
    y_out,
    y_in,
    t_rows,
    first_slot,
    first_count,
    second_slot,
    second_count,
    small_sem,
    load_sem,
    wo_sem,
    x_send,
    x_recv,
    q_send,
    q_recv,
    o_send,
    o_recv,
    st_send,
    st_recv,
    y_send,
    y_recv,
):
    steps, own, cols = states_far.shape
    rows = steps * own
    chunks = cols // HEAD
    width = cols * n_mp
    q_width = w_query.shape[1]
    heads = q_width // HEAD
    group = steps * heads
    slots, block_len, _ = cached_keys.shape
    requests = req_len.shape[0]
    scaling = HEAD**-0.5
    my_seq = lax.axis_index("seq")
    my_mp = lax.axis_index("mp")

    smalls = [
        pltpu.make_async_copy(source, target, small_sem.at[i])
        for i, (source, target) in enumerate(
            (
                (states_far, x_raw.at[lax.axis_index("mp")]),
                (req_len_far, req_len),
                (slot_request_far, slot_request),
                (slot_block_far, slot_block),
                (slot_empty_far, slot_empty),
                (norm_gain_far, norm_gain),
                (query_gain_far, query_gain),
                (key_gain_far, key_gain),
            )
        )
    ]
    for small in smalls:
        small.start()

    barrier = pltpu.get_barrier_semaphore()
    for k in range(1, n_mp):
        pl.semaphore_signal(
            barrier, inc=1, device_id={"mp": flip(my_mp, k, n_mp)}, device_id_type=MESH
        )

    def greet(k, carry):
        pl.semaphore_signal(
            barrier, inc=1, device_id={"seq": flip(my_seq, k, n_seq)}, device_id_type=MESH
        )
        return carry

    loop(1, n_seq, greet, 0)

    loads = [
        pltpu.make_async_copy(w_query, w_all.at[:, 0:q_width], load_sem.at[0]),
        pltpu.make_async_copy(key_matrix, w_all.at[:, q_width : q_width + HEAD], load_sem.at[1]),
        pltpu.make_async_copy(
            value_matrix, w_all.at[:, q_width + HEAD : q_width + 2 * HEAD], load_sem.at[2]
        ),
        pltpu.make_async_copy(cached_keys, k_all, load_sem.at[3]),
        pltpu.make_async_copy(cached_values, v_all, load_sem.at[4]),
    ]
    for k in range(n_mp):
        start = pl.multiple_of(flip(my_mp, k, n_mp) * cols, HEAD)
        loads.append(
            pltpu.make_async_copy(
                w_out.at[:, pl.ds(start, cols)], w_out_parts.at[k], wo_sem.at[k]
            )
        )
    for load in loads[:3]:
        load.start()

    padding = y_out.shape[1] // rows - chunks

    def fold(wide):
        pieces = [wide[:, c * HEAD : (c + 1) * HEAD] for c in range(chunks)]
        pieces += [jnp.zeros((rows, HEAD), F32)] * padding
        return jnp.concatenate(pieces, axis=0).astype(BF16)

    pl.semaphore_wait(barrier, n_mp - 1 + n_seq - 1)

    x_copies = []
    for k in range(n_mp - 1, 0, -1):
        x_copies.append(
            pltpu.make_async_remote_copy(
                src_ref=states_far,
                dst_ref=x_raw.at[my_mp],
                send_sem=x_send.at[k],
                recv_sem=x_recv.at[k],
                device_id={"mp": flip(my_mp, k, n_mp)},
                device_id_type=MESH,
            )
        )
        x_copies[-1].start()
    for small in smalls:
        small.wait()

    owners = []
    for s in range(slots):
        request = slot_request[s]
        used = (slot_empty[s] == 0) & (slot_block[s] * block_len < req_len[request])
        owners.append(jnp.where(used, request, -1))

    def find(b, carry):
        last = jnp.int32(-1)
        earlier = jnp.int32(-1)
        for s in range(slots):
            match = owners[s] == b
            earlier = jnp.where(match, last, earlier)
            last = jnp.where(match, jnp.int32(s), last)
        for found, slot_ref, count_ref in (
            (last, first_slot, first_count),
            (earlier, second_slot, second_count),
        ):
            safe = jnp.maximum(found, 0)
            left = req_len[b] - slot_block[safe] * block_len
            slot_ref[b] = safe
            count_ref[b] = jnp.where(found >= 0, jnp.clip(left, 0, block_len), 0)
        return carry

    lax.fori_loop(0, requests, find, 0)

    row_id = lax.broadcasted_iota(jnp.int32, (rows, HEAD), 0)
    lane_id = lax.broadcasted_iota(jnp.int32, (rows, HEAD), 1)
    position = jnp.zeros((rows, HEAD), jnp.int32)
    for r in range(own):
        length = req_len[my_seq * own + r]
        position = jnp.where(row_id >= r * steps, length + row_id - r * steps, position)
    low_half = lane_id < HEAD // 2
    pair = jnp.where(low_half, lane_id, lane_id - HEAD // 2).astype(F32)
    frequency = jnp.exp(pair * (-2.0 * math.log(ROPE_BASE) / HEAD))
    angle = position.astype(F32) * frequency
    cosine = jnp.cos(angle)
    sine = jnp.sin(angle)
    sine = jnp.where(low_half, -sine, sine)

    def finish_head(values, gain):
        mean = jnp.mean(values * values, axis=-1, keepdims=True)
        values = values * lax.rsqrt(mean + EPS) * gain
        return values * cosine + pltpu.roll(values, HEAD // 2, 1) * sine

    for copy in x_copies:
        copy.wait_recv()
    for m in range(n_mp):
        for t in range(steps):
            block = x_raw[m, t].astype(F32)
            for r in range(own):
                x_rows[r * steps + t : r * steps + t + 1, m * cols : (m + 1) * cols] = block[
                    r : r + 1, :
                ]
    blocks = [x_rows[:, c * HEAD : (c + 1) * HEAD] for c in range(n_mp * chunks)]
    square = sum(piece * piece for piece in blocks)
    mean = jnp.sum(square, axis=-1, keepdims=True) * (1.0 / width)
    factor = lax.rsqrt(mean + EPS)
    gains = norm_gain[...]
    normed = jnp.concatenate(
        [piece * factor * gains[i : i + 1, :] for i, piece in enumerate(blocks)], axis=1
    ).astype(BF16)
    for load in loads[:3]:
        load.wait()
    for load in loads[3:5]:
        load.start()
    projected = jnp.dot(normed, w_all[...], preferred_element_type=F32)

    for h in range(heads):
        one = finish_head(projected[:, h * HEAD : (h + 1) * HEAD], query_gain[...])
        for r in range(own):
            q_rows[r, h * steps : (h + 1) * steps, :] = one[r * steps : (r + 1) * steps, :]
    for r in range(own):
        q_parts[0, r] = q_rows[r].astype(BF16)

    def query_copy(k):
        return pltpu.make_async_remote_copy(
            src_ref=q_parts.at[0],
            dst_ref=q_parts.at[k],
            send_sem=q_send.at[k],
            recv_sem=q_recv.at[k],
            device_id={"seq": flip(my_seq, k, n_seq)},
            device_id_type=MESH,
        )

    def send_query(i, carry):
        query_copy(n_seq - i).start()
        return carry

    loop(1, n_seq, send_query, 0)

    own_keys = finish_head(projected[:, q_width : q_width + HEAD], key_gain[...])
    own_values = projected[:, q_width + HEAD : q_width + 2 * HEAD]
    for source, target in ((own_keys, new_keys), (own_values, new_values)):
        for r in range(own):
            for t in range(steps):
                t_rows[t * own + r : t * own + r + 1, 0:HEAD] = source[
                    r * steps + t : r * steps + t + 1, :
                ]
        for t in range(steps):
            target[t] = t_rows[t * own : (t + 1) * own, 0:HEAD].astype(BF16)
    own_keys = own_keys.astype(BF16)
    own_values = own_values.astype(BF16)

    for load in loads[3:5]:
        load.wait()
    for load in loads[5:]:
        load.start()

    key_lane = lax.broadcasted_iota(jnp.int32, (group, block_len), 1)
    contract = (((1,), (1,)), ((), ()))

    def masked_scores(query, slot, count):
        scores = lax.dot_general(query, k_all[slot], contract, preferred_element_type=F32)
        return jnp.where(key_lane < count, scores * scaling, NEGATIVE)

    def masked_weights(scores, top, count):
        return jnp.where(key_lane < count, jnp.exp(scores - top), 0.0)

    def row_max(values):
        return jnp.max(values, axis=-1, keepdims=True)

    def row_sum(values):
        return jnp.sum(values, axis=-1, keepdims=True)

    fresh_col = lax.broadcasted_iota(jnp.int32, (group, rows), 1)
    fresh_row = lax.broadcasted_iota(jnp.int32, (group, rows), 0) % steps
    state = []
    for r in range(own):
        b = my_seq * own + r
        query = q_parts[0, r]
        one, one_count = first_slot[b], first_count[b]
        two, two_count = second_slot[b], second_count[b]
        score_one = masked_scores(query, one, one_count)
        score_two = masked_scores(query, two, two_count)
        allowed = (fresh_col >= r * steps) & (fresh_col - r * steps <= fresh_row)
        fresh = lax.dot_general(query, own_keys, contract, preferred_element_type=F32)
        fresh = jnp.where(allowed, fresh * scaling, NEGATIVE)
        top = jnp.maximum(jnp.maximum(row_max(score_one), row_max(score_two)), row_max(fresh))
        weight_one = masked_weights(score_one, top, one_count)
        weight_two = masked_weights(score_two, top, two_count)
        weight_new = jnp.where(allowed, jnp.exp(fresh - top), 0.0)
        total = row_sum(weight_one + weight_two) + row_sum(weight_new)
        mix = (
            jnp.dot(weight_one.astype(BF16), v_all[one], preferred_element_type=F32)
            + jnp.dot(weight_two.astype(BF16), v_all[two], preferred_element_type=F32)
            + jnp.dot(weight_new.astype(BF16), own_values, preferred_element_type=F32)
        )
        state += [top, total, mix]

    stat_lane = lax.broadcasted_iota(jnp.int32, (group, HEAD), 1)
    stat_row = lax.broadcasted_iota(jnp.int32, (group, HEAD), 0)
    at_top = stat_lane == stat_row
    at_total = stat_lane == stat_row + HEAD // 2

    def partial_copies(k):
        there = {"seq": flip(my_seq, k, n_seq)}
        return (
            pltpu.make_async_remote_copy(
                src_ref=o_out.at[k],
                dst_ref=o_in.at[k],
                send_sem=o_send.at[k],
                recv_sem=o_recv.at[k],
                device_id=there,
                device_id_type=MESH,
            ),
            pltpu.make_async_remote_copy(
                src_ref=st_out.at[k],
                dst_ref=st_in.at[k],
                send_sem=st_send.at[k],
                recv_sem=st_recv.at[k],
                device_id=there,
                device_id_type=MESH,
            ),
        )

    def serve(ks):
        jobs = []
        for k in ks:
            query_copy(k).wait_recv()
        for k in ks:
            peer = flip(my_seq, k, n_seq)
            for r in range(own):
                b = peer * own + r
                jobs.append((k, r, first_slot[b], first_count[b]))
        scores = [masked_scores(q_parts[k, r], slot, count) for k, r, slot, count in jobs]
        tops = [row_max(score) for score in scores]
        weights = [
            masked_weights(score, top, job[3]) for score, top, job in zip(scores, tops, jobs)
        ]
        totals = [row_sum(weight) for weight in weights]
        lines = []
        for (k, r, slot, _), weight, top, total in zip(jobs, weights, tops, totals):
            mix = jnp.dot(weight.astype(BF16), v_all[slot], preferred_element_type=F32)
            o_out[k, r] = mix.astype(BF16)
            spread = jnp.where(at_top, top, jnp.where(at_total, total, 0.0))
            lines.append(jnp.sum(spread, axis=0, keepdims=True))
        for line, (k, r, _, _) in zip(lines, jobs):
            st_out[k, r : r + 1, :] = line
        for k in ks:
            for copy in partial_copies(k):
                copy.start()

    def merge(ks, carry):
        for k in ks:
            for copy in partial_copies(k):
                copy.wait_recv()
        carry = list(carry)
        for r in range(own):
            tops, totals, mixes = ([item] for item in carry[3 * r : 3 * r + 3])
            for k in ks:
                line = jnp.broadcast_to(st_in[k, r : r + 1, :], (group, HEAD))
                tops.append(row_sum(jnp.where(at_top, line, 0.0)))
                totals.append(row_sum(jnp.where(at_total, line, 0.0)))
                mixes.append(o_in[k, r].astype(F32))
            overall = functools.reduce(jnp.maximum, tops)
            factors = [jnp.exp(top - overall) for top in tops]
            carry[3 * r] = overall
            carry[3 * r + 1] = sum(total * f for total, f in zip(totals, factors))
            carry[3 * r + 2] = sum(mix * f for mix, f in zip(mixes, factors))
        return tuple(carry)

    state = tuple(state)
    if n_seq <= UNROLL_UP_TO:
        groups = [range(1, n_seq // 2), range(n_seq // 2, n_seq)]
        for ks in groups:
            serve(ks)
        for ks in groups:
            state = merge(ks, state)
    else:

        def serve_one(k, carry):
            serve([k])
            return carry

        lax.fori_loop(1, n_seq, serve_one, 0)
        state = lax.fori_loop(1, n_seq, lambda k, carry: merge([k], carry), state)

    for r in range(own):
        attended = state[3 * r + 2] / state[3 * r + 1]
        for h in range(heads):
            att_rows[r * steps : (r + 1) * steps, h * HEAD : (h + 1) * HEAD] = attended[
                h * steps : (h + 1) * steps, :
            ]
    attended = att_rows[...].astype(BF16)

    y_copies = []
    for k in range(n_mp - 1, 0, -1):
        loads[5 + k].wait()
        y_out[k] = fold(jnp.dot(attended, w_out_parts[k], preferred_element_type=F32))
        y_copies.append(
            pltpu.make_async_remote_copy(
                src_ref=y_out.at[k],
                dst_ref=y_in.at[k],
                send_sem=y_send.at[k],
                recv_sem=y_recv.at[k],
                device_id={"mp": flip(my_mp, k, n_mp)},
                device_id_type=MESH,
            )
        )
        y_copies[-1].start()
    loads[5].wait()
    summed = jnp.dot(attended, w_out_parts[0], preferred_element_type=F32)
    own_start = pl.multiple_of(my_mp * cols, HEAD)
    summed = x_rows[:, pl.ds(own_start, cols)] + summed

    for copy in x_copies:
        copy.wait_send()

    def drain(k, carry):
        query_copy(k).wait_send()
        for copy in partial_copies(k):
            copy.wait_send()
        return carry

    loop(1, n_seq, drain, 0)

    for copy in y_copies:
        copy.wait_recv()
    for k in range(1, n_mp):
        folded = y_in[k].astype(F32)
        summed = summed + jnp.concatenate(
            [folded[c * rows : (c + 1) * rows, :] for c in range(chunks)], axis=1
        )
    for r in range(own):
        for t in range(steps):
            t_rows[t * own + r : t * own + r + 1, :] = summed[
                r * steps + t : r * steps + t + 1, :
            ]
    for t in range(steps):
        hidden[t] = t_rows[t * own : (t + 1) * own, :].astype(BF16)
    for copy in y_copies:
        copy.wait_send()


def write_out(*refs):
    count = len(refs) // 2
    sem = refs[-1]
    copies = [
        pltpu.make_async_copy(refs[i], refs[count + i], sem.at[i]) for i in range(count)
    ]
    for copy in copies:
        copy.start()
    for copy in copies:
        copy.wait()


def shards(n_seq, n_mp, *args):
    (
        states,
        norm_gain,
        query_gain,
        key_gain,
        w_query,
        key_matrix,
        value_matrix,
        w_out,
        cached_keys,
        cached_values,
        req_len,
        slot_request,
        slot_block,
        slot_empty,
    ) = args
    steps, own, cols = states.shape
    width, q_width = w_query.shape
    heads = q_width // HEAD
    group = steps * heads
    rows = steps * own
    slots, block_len, _ = cached_keys.shape
    requests = req_len.shape[0]
    assert key_matrix.shape[1] == HEAD
    part_rows = -(-(rows * (cols // HEAD)) // 16) * 16
    vmem = pl.BlockSpec(memory_space=pltpu.VMEM)
    far = pl.BlockSpec(memory_space=pltpu.HBM)
    dma = pltpu.SemaphoreType.DMA
    results = pl.pallas_call(
        functools.partial(kernel, n_seq, n_mp),
        out_shape=(
            pltpu.VMEM(states.shape, BF16),
            pltpu.VMEM((steps, own, HEAD), BF16),
            pltpu.VMEM((steps, own, HEAD), BF16),
        ),
        in_specs=[far] * 14,
        out_specs=(vmem, vmem, vmem),
        scratch_shapes=[
            pltpu.VMEM((n_mp,) + states.shape, BF16),
            pltpu.VMEM((width // HEAD, HEAD), F32),
            pltpu.VMEM((1, HEAD), F32),
            pltpu.VMEM((1, HEAD), F32),
            pltpu.SMEM((requests,), jnp.int32),
            pltpu.SMEM((slots,), jnp.int32),
            pltpu.SMEM((slots,), jnp.int32),
            pltpu.SMEM((slots,), jnp.int32),
            pltpu.VMEM((rows, width), F32),
            pltpu.VMEM((width, q_width + 2 * HEAD), BF16),
            pltpu.VMEM((n_mp, q_width, cols), BF16),
            pltpu.VMEM((slots, block_len, HEAD), BF16),
            pltpu.VMEM((slots, block_len, HEAD), BF16),
            pltpu.VMEM((own, group, HEAD), F32),
            pltpu.VMEM((n_seq, own, group, HEAD), BF16),
            pltpu.VMEM((n_seq, own, group, HEAD), BF16),
            pltpu.VMEM((n_seq, own, group, HEAD), BF16),
            pltpu.VMEM((n_seq, own, HEAD), F32),
            pltpu.VMEM((n_seq, own, HEAD), F32),
            pltpu.VMEM((rows, q_width), F32),
            pltpu.VMEM((n_mp, part_rows, HEAD), BF16),
            pltpu.VMEM((n_mp, part_rows, HEAD), BF16),
            pltpu.VMEM((rows, cols), F32),
            pltpu.SMEM((requests,), jnp.int32),
            pltpu.SMEM((requests,), jnp.int32),
            pltpu.SMEM((requests,), jnp.int32),
            pltpu.SMEM((requests,), jnp.int32),
            dma((8,)),
            dma((5,)),
            dma((n_mp,)),
            dma((n_mp,)),
            dma((n_mp,)),
            dma((n_seq,)),
            dma((n_seq,)),
            dma((n_seq,)),
            dma((n_seq,)),
            dma((n_seq,)),
            dma((n_seq,)),
            dma((n_mp,)),
            dma((n_mp,)),
        ],
        compiler_params=pltpu.CompilerParams(
            collective_id=0, has_side_effects=True, vmem_limit_bytes=63 * 1024 * 1024
        ),
    )(
        states,
        norm_gain.reshape(-1, HEAD),
        query_gain.reshape(1, -1),
        key_gain.reshape(1, -1),
        w_query,
        key_matrix,
        value_matrix,
        w_out,
        cached_keys,
        cached_values,
        req_len,
        slot_request,
        slot_block,
        slot_empty,
    )
    return pl.pallas_call(
        write_out,
        out_shape=tuple(jax.ShapeDtypeStruct(x.shape, x.dtype) for x in results),
        in_specs=[vmem] * 3,
        out_specs=(far,) * 3,
        scratch_shapes=[dma((3,))],
        compiler_params=pltpu.CompilerParams(vmem_limit_bytes=1024 * 1024),
    )(*results)


def solution(mesh):
    placed = (
        P(None, "seq", "mp"),
        P(),
        P(),
        P(),
        P(None, "mp"),
        P(None, "mp"),
        P(None, "mp"),
        P("mp", None),
        P("seq", None, "mp"),
        P("seq", None, "mp"),
        P(),
        P("seq"),
        P("seq"),
        P("seq"),
    )
    return jax.shard_map(
        functools.partial(shards, mesh.shape["seq"], mesh.shape["mp"]),
        mesh=mesh,
        in_specs=placed,
        out_specs=(P(None, "seq", "mp"), P(None, "seq", "mp"), P(None, "seq", "mp")),
        check_vma=False,
    )
```
